256 devices in a mesh: seq: 32 (over y_hi, z, core), head: 8 (over x, y_lo).
Axes of the slice: x: 4, y: 4 (y_hi: 2, y_lo: 2; y = y_hi * 2 + y_lo), z: 8, core: 2. Of those that a mesh axis runs over, the one named last changes fastest.
Arguments:
- q1: bfloat16 [8192, 6144], P('seq', 'head'), may hold values from -6 to 6
- k1: bfloat16 [8192, 6144], P('seq', 'head'), may hold values from -6 to 6
- v1: bfloat16 [8192, 6144], P('seq', 'head'), may hold values from -6 to 6
- decay1: float32 [8192, 48], P('seq', 'head'), may hold values from -1 to 0, as said below
- gain_out1: float32 [6144], P('head'), may hold values from 0.25 to 1.75
- wo1: bfloat16 [6144, 3072], P('head'), may hold values from -0.109375 to 0.109375
- stream_in: bfloat16 [8192, 3072], P('seq', 'head'), may hold values from -20 to 20
- gain_in2: float32 [3072], replicated, may hold values from 0.25 to 1.75
- wq2: bfloat16 [3072, 6144], P('seq', 'head'), may hold values from -0.109375 to 0.109375
- wk2: bfloat16 [3072, 6144], P('seq', 'head'), may hold values from -0.109375 to 0.109375
- wv2: bfloat16 [3072, 6144], P('seq', 'head'), may hold values from -0.109375 to 0.109375
- decay2: float32 [8192, 48], P('seq', 'head'), may hold values from -1 to 0, as said below
- gain_out2: float32 [6144], P('head'), may hold values from 0.25 to 1.75
- wo2: bfloat16 [6144, 3072], P('head'), may hold values from -0.109375 to 0.109375
Outputs:
- mixed: bfloat16 [8192, 3072], P('seq', 'head')
The draws below stay inside these ranges and needn't reach their ends.
Inputs may be any that keep to these rules, and one draw needn't show every extreme that they name: `decay1`: every value is negative. `decay2`: every value is negative.
All inputs are finite; a program needn't handle non-finite values.
Results may differ from the reference program's by a relative error of at most 0.02.
Values may be sent and summed in bfloat16 or wider, within the bound.
No kernel may reach another device: no remote copies, remote signals or barrier semaphores. Data moves between devices by JAX's collectives and lax.ppermute only.
A program may use at most 128 MiB of HBM per device.

```python
import math
import jax
import jax.numpy as jnp
from jax import lax

D = 3072
HEADS = 48
DH = 128
TOK_DEV = 256
HD = 6144
TOKEN_COUNT = 8192
N_SEQ = 32


def decay_law(key, slow_share):
    random_subkeys = jax.random.split(key, 7)
    slow_heads = jax.random.uniform(random_subkeys[0], (HEADS,)) < slow_share
    fast_rate = jnp.exp(jax.random.uniform(random_subkeys[1], (HEADS,), minval=math.log(1.0 / 50.0), maxval=math.log(1.0 / 20.0)))
    slow_rate = jax.random.uniform(random_subkeys[2], (HEADS,), minval=0.2, maxval=0.8) / TOKEN_COUNT
    decay_speed = jnp.where(slow_heads, slow_rate, fast_rate)
    block_multiplier = jnp.exp(jax.random.uniform(random_subkeys[3], (TOKEN_COUNT // TOK_DEV, 1), minval=-0.7, maxval=0.7))
    block_multiplier = jnp.repeat(block_multiplier, TOK_DEV, axis=0)
    approximate_result = jnp.exp(jax.random.uniform(random_subkeys[4], (TOKEN_COUNT, HEADS), minval=-0.7, maxval=0.7))
    segment_rows = jax.random.randint(random_subkeys[5], (2,), 0, TOKEN_COUNT)
    segment_retained = jax.random.uniform(random_subkeys[6], (2,), minval=0.55, maxval=0.8)
    token_positions = jnp.arange(TOKEN_COUNT)
    segment_list = jnp.where(token_positions == segment_rows[0], jnp.log(segment_retained[0]), 0.0)
    segment_list = segment_list + jnp.where(token_positions == segment_rows[1], jnp.log(segment_retained[1]), 0.0)
    value_rows = -decay_speed[None, :] * block_multiplier * approximate_result + segment_list[:, None]
    return value_rows.astype(jnp.float32)


def draw_decay1(key, part):
    key = jax.random.fold_in(key, 21)
    share = 0.5
    return decay_law(key, share)


def draw_decay2(key, part):
    key = jax.random.fold_in(key, 22)
    share = 0.5
    return decay_law(key, share)


def draw_stream_in(key, part):
    key = jax.random.fold_in(key, 11)
    scale_key, value_key = jax.random.split(key)
    row_scale = jnp.exp(jax.random.uniform(scale_key, (TOKEN_COUNT, 1), minval=math.log(0.5), maxval=math.log(5.0)))
    value_rows = jnp.clip(jax.random.normal(value_key, (TOKEN_COUNT, D)), -4.0, 4.0)
    return (value_rows * row_scale).astype(jnp.float32).astype(jnp.bfloat16)


def raised(result, rng, source, target, parts, factor):
    owner, partner = [(jnp.arange(result.shape[axis_at]) // (result.shape[axis_at] // parts)).reshape([-1 if axis == axis_at else 1 for axis in range(result.ndim)]) for axis_at in (source, target)]
    chosen = jax.random.permutation(rng, parts)[partner]
    strong = (owner == chosen) | (owner == (partner + parts // 2) % parts)
    return jnp.where(strong, factor * result, result)


def level_of(rng, shape, cuts, least, top_value):
    level = 1.0
    for axis_at, blocks in cuts:
        steps = jax.random.uniform(jax.random.fold_in(jax.random.fold_in(rng, 6), axis_at), (blocks,), jnp.float32, least / len(cuts), top_value / len(cuts))
        level = level * jnp.repeat(jnp.exp(steps), shape[axis_at] // blocks).reshape((-1,) + (1,) * (len(shape) - 1 - axis_at))
    return level


def scatter_about(stream_key, dims, scale, limit, shards=(), held_as=jnp.bfloat16):
    entries = jax.random.normal(stream_key, dims, jnp.float32) * scale
    if len(shards) > 0:
        entries = level_of(stream_key, dims, shards, -0.22, 0.18) * entries
    return jnp.clip(entries, min=-limit, max=limit).astype(held_as)


def bell_draw_with(own_key, dims, scale, reach, shards, heavy, held_as=jnp.bfloat16):
    values = scale * jax.random.normal(own_key, dims, jnp.float32)
    if shards:
        values = values * level_of(own_key, dims, shards, -0.22, 0.18)
    return jnp.clip(raised(values, jax.random.fold_in(own_key, 3), *heavy), -reach, reach).astype(held_as)


def setup_inputs(seed: int = 0) -> dict:
    arg_keys = jax.random.split(jax.random.key(seed), 15)
    q1 = scatter_about(arg_keys[0], (TOKEN_COUNT, HD), 1.0, 6.0, ((0, 32), (1, 8)))
    k1 = scatter_about(arg_keys[1], (TOKEN_COUNT, HD), 1.0, 6.0, ((0, 32), (1, 8)))
    v1 = scatter_about(arg_keys[2], (TOKEN_COUNT, HD), 1.0, 6.0, ((0, 32), (1, 8)))
    decay1 = draw_decay1(jax.random.fold_in(arg_keys[14], 71), 0)
    gain_out1 = jnp.clip(1.0 + 0.15 * jax.random.normal(arg_keys[4], (HD,), jnp.float32), 0.25, 1.75)
    wo1 = bell_draw_with(arg_keys[5], (HD, D), HD ** -0.5, 0.109375, ((0, 8),), (0, 1, 8, 2.0))
    stream_in = draw_stream_in(jax.random.fold_in(arg_keys[14], 71), 0)
    gain_in2 = jnp.clip(1.0 + 0.15 * jax.random.normal(arg_keys[7], (D,), jnp.float32), 0.25, 1.75)
    wq2 = scatter_about(arg_keys[8], (D, HD), D ** -0.5, 0.109375, ((0, 32), (1, 8)))
    wk2 = scatter_about(arg_keys[9], (D, HD), D ** -0.5, 0.109375, ((0, 32), (1, 8)))
    wv2 = scatter_about(arg_keys[10], (D, HD), D ** -0.5, 0.109375, ((0, 32), (1, 8)))
    decay2 = draw_decay2(jax.random.fold_in(arg_keys[14], 71), 0)
    gain_out2 = jnp.clip(1.0 + 0.15 * jax.random.normal(arg_keys[12], (HD,), jnp.float32), 0.25, 1.75)
    wo2 = bell_draw_with(arg_keys[13], (HD, D), HD ** -0.5, 0.109375, ((0, 8),), (0, 1, 8, 2.0))
    return dict(q1=q1, k1=k1, v1=v1, decay1=decay1, gain_out1=gain_out1, wo1=wo1, stream_in=stream_in, gain_in2=gain_in2, wq2=wq2, wk2=wk2, wv2=wv2, decay2=decay2, gain_out2=gain_out2, wo2=wo2)


def silu_round(value_rows):
    wide = value_rows.astype(jnp.float32)
    return jax.nn.silu(wide).astype(jnp.bfloat16)

def block_attend(state, inputs):
    query_act, key_act, value_act, log_decay = inputs
    cumdecay = jnp.cumsum(log_decay, axis=0)
    across = cumdecay.T
    rows_here = query_act.shape[0]
    lower = (jnp.arange(rows_here)[:, None] >= jnp.arange(rows_here)[None, :])[None]
    spread = across[:, :, None] - across[:, None, :]
    factor = jnp.where(lower, jnp.exp(jnp.where(lower, spread, 0.0)), 0.0)
    scores = jnp.einsum('thd,shd->hts', query_act.astype(jnp.float32), key_act.astype(jnp.float32))
    weights = (scores * factor).astype(jnp.bfloat16)
    intra = jnp.einsum('hts,shd->thd', weights.astype(jnp.float32), value_act.astype(jnp.float32))
    carried = jnp.einsum('thd,hde->the', query_act.astype(jnp.float32), state, precision=lax.Precision.HIGHEST) * jnp.exp(cumdecay)[:, :, None]
    last_total = across[:, -1]
    tail = jnp.exp(last_total[None, :] - cumdecay)
    local_state = jnp.einsum('thd,the->hde', key_act.astype(jnp.float32) * tail[:, :, None], value_act.astype(jnp.float32), precision=lax.Precision.HIGHEST)
    new_state = jnp.exp(last_total)[:, None, None] * state + local_state
    return (new_state, intra + carried)

def attend(query_pre, key_pre, value_pre, log_decay, gain):
    query_act = silu_round(query_pre).reshape(N_SEQ, TOK_DEV, HEADS, DH)
    key_act = silu_round(key_pre).reshape(N_SEQ, TOK_DEV, HEADS, DH)
    value_act = silu_round(value_pre).reshape(N_SEQ, TOK_DEV, HEADS, DH)
    decay_blocks = log_decay.reshape(N_SEQ, TOK_DEV, HEADS)
    start_state = jnp.zeros((HEADS, DH, DH), jnp.float32)
    final_state, att = lax.scan(block_attend, start_state, (query_act, key_act, value_act, decay_blocks))
    att = att.reshape(TOKEN_COUNT, HEADS, DH)
    mean_square = lax.optimization_barrier(jnp.mean(att * att, axis=-1, keepdims=True))
    normed = att * lax.rsqrt(mean_square + 1e-06) * gain.reshape(HEADS, DH)
    return normed.reshape(TOKEN_COUNT, HD).astype(jnp.bfloat16)

def reference(q1, k1, v1, decay1, gain_out1, wo1, stream_in, gain_in2, wq2, wk2, wv2, decay2, gain_out2, wo2):
    first_out = attend(q1, k1, v1, decay1, gain_out1)
    stream = (stream_in.astype(jnp.float32) + jnp.dot(first_out, wo1, preferred_element_type=jnp.float32)).astype(jnp.bfloat16)
    wide = stream.astype(jnp.float32)
    normed = wide * lax.rsqrt(lax.optimization_barrier(jnp.mean(wide * wide, axis=-1, keepdims=True)) + 1e-06) * gain_in2
    inputs = normed.astype(jnp.bfloat16)
    query_pre = jnp.dot(inputs, wq2, preferred_element_type=jnp.float32)
    key_pre = jnp.dot(inputs, wk2, preferred_element_type=jnp.float32)
    value_pre = jnp.dot(inputs, wv2, preferred_element_type=jnp.float32)
    second_out = attend(query_pre, key_pre, value_pre, decay2, gain_out2)
    return (stream.astype(jnp.float32) + jnp.dot(second_out, wo2, preferred_element_type=jnp.float32)).astype(jnp.bfloat16)
```

```python
import functools

import jax
import jax.numpy as jnp
from jax import lax
from jax.experimental import pallas as pl
from jax.experimental.pallas import tpu as pltpu
from jax.sharding import Mesh
from jax.sharding import PartitionSpec as P

DH = 128
BLK = 256
TOK = 512
HC = 3
HW = HC * DH
NCHIP = 16
SUB = DH // NCHIP
PIECE = 32
WIDTH = 384
NHEAD = 8
SWAP = [(0, 1), (1, 0)]
VMEM = 40 * 1024 * 1024


def silu(u):
    return u / (1.0 + jnp.exp(-u))


def attn_core(qs, ks, vs, dec, pieces_ref, intra_ref, cum_ref):
    row = lax.broadcasted_iota(jnp.int32, (TOK, TOK), 0)
    col = lax.broadcasted_iota(jnp.int32, (TOK, TOK), 1)
    tri = (row >= col).astype(jnp.float32)
    cum = jnp.dot(tri, dec, preferred_element_type=jnp.float32, precision=lax.Precision.HIGHEST)
    cum_ref[...] = cum
    across = cum.T
    lower = lax.broadcasted_iota(jnp.int32, (BLK, BLK), 0) >= lax.broadcasted_iota(
        jnp.int32, (BLK, BLK), 1
    )
    states = []
    decays = jnp.zeros((SUB, DH), jnp.float32)
    slot = lax.broadcasted_iota(jnp.int32, (SUB, DH), 0)
    for h in range(HC):
        cols = slice(h * DH, (h + 1) * DH)
        q, k, v = qs[:, cols], ks[:, cols], vs[:, cols]
        ch = cum[:, h : h + 1]
        rh = across[h : h + 1, :]
        for i in range(2):
            rows = slice(i * BLK, (i + 1) * BLK)
            parts = []
            for j in range(i + 1):
                keys = slice(j * BLK, (j + 1) * BLK)
                scores = lax.dot_general(
                    q[rows], k[keys], (((1,), (1,)), ((), ())), preferred_element_type=jnp.float32
                )
                spread = ch[rows] - rh[:, keys]
                if i == j:
                    factor = jnp.where(lower, jnp.exp(jnp.where(lower, spread, 0.0)), 0.0)
                else:
                    factor = jnp.exp(spread)
                weights = (scores * factor).astype(jnp.bfloat16)
                parts.append(jnp.dot(weights, v[keys], preferred_element_type=jnp.float32))
            intra_ref[rows, cols] = parts[0] if i == 0 else parts[0] + parts[1]
        last = cum[TOK - 1 : TOK, h : h + 1]
        kt = (k.astype(jnp.float32) * jnp.exp(last - ch)).astype(jnp.bfloat16)
        state = lax.dot_general(
            kt, v, (((0,), (0,)), ((), ())), preferred_element_type=jnp.float32
        )
        states.append(state.reshape(NCHIP, SUB, DH))
        total = jnp.exp(last)
        high = total.astype(jnp.bfloat16).astype(jnp.float32)
        decays = jnp.where(slot == h, high, decays)
        decays = jnp.where(slot == HC + h, total - high, decays)
    states.append(jnp.broadcast_to(decays[None], (NCHIP, SUB, DH)))
    pieces_ref[...] = jnp.concatenate(states, axis=1).astype(jnp.bfloat16)


def first_kernel(place, q_ref, k_ref, v_ref, other_ref, dec_ref, pieces_ref, intra_ref, cum_ref, qs, ks, vs):
    core = place[0]
    mine = pl.ds(pl.multiple_of(core * BLK, BLK), BLK)
    yours = pl.ds(pl.multiple_of((1 - core) * BLK, BLK), BLK)
    cols = pl.ds(pl.multiple_of(core * HW, DH), HW)
    for n, (src, dst) in enumerate(((q_ref, qs), (k_ref, ks), (v_ref, vs))):
        dst[mine, :] = silu(src[:, cols].astype(jnp.float32)).astype(jnp.bfloat16)
        dst[yours, :] = silu(other_ref[:, n * HW : (n + 1) * HW].astype(jnp.float32)).astype(
            jnp.bfloat16
        )
    attn_core(qs, ks, vs, dec_ref[...], pieces_ref, intra_ref, cum_ref)


def core_outs():
    return (
        jax.ShapeDtypeStruct((NCHIP, PIECE, DH), jnp.bfloat16),
        jax.ShapeDtypeStruct((TOK, HW), jnp.float32),
        jax.ShapeDtypeStruct((TOK, DH), jnp.float32),
        jax.ShapeDtypeStruct((TOK, HW), jnp.bfloat16),
    )


def whole(shape):
    return pl.BlockSpec(shape, lambda *_: (0,) * len(shape))


def first_prep(place, q, k, v, other, dec):
    outs = core_outs()
    return pl.pallas_call(
        first_kernel,
        out_shape=outs,
        grid_spec=pltpu.PrefetchScalarGridSpec(
            num_scalar_prefetch=1,
            grid=(1,),
            in_specs=[whole(a.shape) for a in (q, k, v, other, dec)],
            out_specs=[whole(o.shape) for o in outs],
            scratch_shapes=[pltpu.VMEM((TOK, HW), jnp.bfloat16)] * 2,
        ),
        compiler_params=pltpu.CompilerParams(vmem_limit_bytes=VMEM),
        name="first_prep",
    )(place, q, k, v, other, dec)


def second_kernel(
    place, mine_ref, yours_ref, wa_ref, wb_ref, gain_ref, dec_ref,
    pieces_ref, intra_ref, cum_ref, qs, ks, vs, scale, acc,
):
    core, side = place[0], place[1]
    step = pl.program_id(0)
    half = NHEAD // 2

    @pl.when(step == 0)
    def _():
        for n, src in enumerate((mine_ref, yours_ref)):
            total = jnp.zeros((BLK, 1), jnp.float32)
            for i in range(NHEAD):
                wide = src[i].astype(jnp.float32)
                total = total + jnp.sum(wide * wide, axis=-1, keepdims=True)
            root = lax.rsqrt(total / (NHEAD * WIDTH) + 1e-06)
            scale[n * BLK : (n + 1) * BLK, :] = jnp.broadcast_to(root, (BLK, DH))
        acc[...] = jnp.zeros_like(acc)

    chunk = jnp.where(step < half, side * half + step, (1 - side) * half + step - half)
    gain = gain_ref[chunk]

    def normed(src, n):
        root = scale[n * BLK : (n + 1) * BLK, 0:1]
        return (src[chunk].astype(jnp.float32) * root * gain).astype(jnp.bfloat16)

    rows = jnp.concatenate([normed(mine_ref, 0), normed(yours_ref, 1)], axis=0)

    @pl.when(step < half)
    def _():
        acc[...] += jnp.dot(rows, wa_ref[...], preferred_element_type=jnp.float32)

    @pl.when(step >= half)
    def _():
        acc[...] += jnp.dot(rows, wb_ref[...], preferred_element_type=jnp.float32)

    @pl.when(step == NHEAD - 1)
    def _():
        first = pl.ds(pl.multiple_of(core * BLK, BLK), BLK)
        second = pl.ds(pl.multiple_of((1 - core) * BLK, BLK), BLK)
        for n, dst in enumerate((ks, vs, qs)):
            cols = slice(n * HW, (n + 1) * HW)
            dst[first, :] = silu(acc[:BLK, cols]).astype(jnp.bfloat16)
            dst[second, :] = silu(acc[BLK:, cols]).astype(jnp.bfloat16)
        attn_core(qs, ks, vs, dec_ref[...], pieces_ref, intra_ref, cum_ref)


def second_prep(place, mine, yours, wa, wb, gain, dec):
    outs = core_outs()
    half = NHEAD // 2
    return pl.pallas_call(
        second_kernel,
        out_shape=outs,
        grid_spec=pltpu.PrefetchScalarGridSpec(
            num_scalar_prefetch=1,
            grid=(NHEAD,),
            in_specs=[
                whole(mine.shape),
                whole(yours.shape),
                pl.BlockSpec((WIDTH, 3 * HW), lambda i, *_: (jnp.minimum(i, half - 1), 0)),
                pl.BlockSpec((WIDTH, 3 * HW), lambda i, *_: (jnp.maximum(i - half, 0), 0)),
                whole(gain.shape),
                whole(dec.shape),
            ],
            out_specs=[whole(o.shape) for o in outs],
            scratch_shapes=[
                pltpu.VMEM((TOK, HW), jnp.bfloat16),
                pltpu.VMEM((TOK, HW), jnp.bfloat16),
                pltpu.VMEM((TOK, DH), jnp.float32),
                pltpu.VMEM((TOK, 3 * HW), jnp.float32),
            ],
        ),
        compiler_params=pltpu.CompilerParams(vmem_limit_bytes=VMEM),
        name="second_prep",
    )(place, mine, yours, wa, wb, gain, dec)


def scan_kernel(in_ref, out_ref):
    states = [jnp.zeros((SUB, DH), jnp.float32) for _ in range(HC)]
    empty = jnp.zeros((PIECE - HC * SUB, DH), jnp.float32)
    for p in range(NCHIP):
        piece = in_ref[p].astype(jnp.float32)
        out_ref[p] = jnp.concatenate(states + [empty], axis=0).astype(jnp.bfloat16)
        decays = piece[HC * SUB :]
        for h in range(HC):
            decay = decays[h : h + 1] + decays[HC + h : HC + h + 1]
            states[h] = states[h] * decay + piece[h * SUB : (h + 1) * SUB]


def scan(pieces):
    return pl.pallas_call(
        scan_kernel,
        out_shape=jax.ShapeDtypeStruct(pieces.shape, pieces.dtype),
        name="scan",
    )(pieces)


def finish_kernel(place, pieces_ref, intra_ref, cum_ref, qs_ref, gain_ref, mine_ref, yours_ref, out):
    core = place[0]
    pieces = pieces_ref[...].astype(jnp.float32)
    for h in range(HC):
        cols = slice(h * DH, (h + 1) * DH)
        state = pieces[:, h * SUB : (h + 1) * SUB].reshape(DH, DH).astype(jnp.bfloat16)
        carried = jnp.dot(qs_ref[:, cols], state, preferred_element_type=jnp.float32)
        att = intra_ref[:, cols] + carried * jnp.exp(cum_ref[:, h : h + 1])
        square = jnp.mean(att * att, axis=-1, keepdims=True)
        out[:, cols] = (att * lax.rsqrt(square + 1e-06) * gain_ref[:, cols]).astype(jnp.bfloat16)
    mine_ref[...] = out[pl.ds(pl.multiple_of(core * BLK, BLK), BLK), :]
    yours_ref[...] = out[pl.ds(pl.multiple_of((1 - core) * BLK, BLK), BLK), :]


def finish(place, pieces, intra, cum, qs, gain):
    args = (pieces, intra, cum, qs, gain)
    return pl.pallas_call(
        finish_kernel,
        out_shape=(jax.ShapeDtypeStruct((BLK, HW), jnp.bfloat16),) * 2,
        grid_spec=pltpu.PrefetchScalarGridSpec(
            num_scalar_prefetch=1,
            grid=(1,),
            in_specs=[whole(a.shape) for a in args],
            out_specs=[whole((BLK, HW))] * 2,
            scratch_shapes=[pltpu.VMEM((TOK, HW), jnp.bfloat16)],
        ),
        compiler_params=pltpu.CompilerParams(vmem_limit_bytes=VMEM),
        name="finish",
    )(place, *args)


def project_kernel(place, mine_ref, yours_ref, w_ref, out_ref):
    core = place[0]
    top = pl.ds(pl.multiple_of(core * HW, DH), HW)
    low = pl.ds(pl.multiple_of((1 - core) * HW, DH), HW)
    term = jnp.dot(mine_ref[...], w_ref[top, :], preferred_element_type=jnp.float32)
    term = term + jnp.dot(yours_ref[...], w_ref[low, :], preferred_element_type=jnp.float32)
    out_ref[0] = term.astype(jnp.bfloat16)


def project(place, mine, yours, w):
    return pl.pallas_call(
        project_kernel,
        out_shape=jax.ShapeDtypeStruct((NHEAD, BLK, WIDTH), jnp.bfloat16),
        grid_spec=pltpu.PrefetchScalarGridSpec(
            num_scalar_prefetch=1,
            grid=(NHEAD,),
            in_specs=[
                whole(mine.shape),
                whole(yours.shape),
                pl.BlockSpec((2 * HW, WIDTH), lambda i, *_: (0, i)),
            ],
            out_specs=pl.BlockSpec((1, BLK, WIDTH), lambda i, *_: (i, 0, 0)),
        ),
        compiler_params=pltpu.CompilerParams(vmem_limit_bytes=VMEM),
        name="project",
    )(place, mine, yours, w)


def exchange(parts, axes):
    return lax.all_to_all(parts, axes, 0, 0)


def rest(place, prepared, gain, w):
    pieces, intra, cum, qs = prepared
    before = exchange(scan(exchange(pieces, ("yh", "z"))), ("yh", "z"))
    mine, yours = finish(place, before, intra, cum, qs, gain)
    yours = lax.ppermute(yours, "c", SWAP)
    terms = exchange(project(place, mine, yours, w), ("x", "yl"))
    return jnp.sum(terms.astype(jnp.float32), axis=0)


def local(
    q1, k1, v1, decay1, gain_out1, wo1, stream_in, gain_in2, wq2, wk2, wv2, decay2, gain_out2, wo2
):
    core = lax.axis_index("c")
    place = jnp.stack([core, lax.axis_index("yh")]).astype(jnp.int32)

    def cut(arrays, which):
        return jnp.concatenate(
            [lax.dynamic_slice_in_dim(a, which * HW, HW, axis=1) for a in arrays], axis=1
        )

    def in_order(own, other):
        first = jnp.where(core == 0, own, other)
        second = jnp.where(core == 0, other, own)
        return jnp.concatenate([first, second], axis=0)

    weights = (wk2, wv2, wq2)
    other_w = lax.ppermute(cut(weights, 1 - core), "c", SWAP)
    chip_w = in_order(cut(weights, core), other_w)
    far_w = lax.ppermute(chip_w, "yh", SWAP)
    wa = lax.all_gather(chip_w, "z", axis=0, tiled=True)
    wb = lax.all_gather(far_w, "z", axis=0, tiled=True)

    other = lax.ppermute(cut((q1, k1, v1), 1 - core), "c", SWAP)
    both = jnp.concatenate([decay1, decay2], axis=1)
    decays = in_order(both, lax.ppermute(both, "c", SWAP))

    def lanes(start):
        part = lax.dynamic_slice_in_dim(decays, start, HC, axis=1)
        return jnp.pad(part, ((0, 0), (0, DH - HC)))

    def own_gain(gain):
        return lax.dynamic_slice_in_dim(gain, core * HW, HW, axis=0)[None]

    prepared = first_prep(place, q1, k1, v1, other, lanes(core * HC))
    first_share = rest(place, prepared, own_gain(gain_out1), wo1)
    stream = (stream_in.astype(jnp.float32) + first_share).astype(jnp.bfloat16)
    mine = exchange(jnp.broadcast_to(stream[None], (NHEAD, BLK, WIDTH)), ("x", "yl"))
    yours = lax.ppermute(mine, "c", SWAP)
    prepared = second_prep(
        place, mine, yours, wa, wb, gain_in2.reshape(NHEAD, 1, WIDTH), lanes(2 * HC + core * HC)
    )
    second_share = rest(place, prepared, own_gain(gain_out2), wo2)
    return (stream.astype(jnp.float32) + second_share).astype(jnp.bfloat16)


def solution(mesh):
    fine = Mesh(mesh.devices.reshape(2, 8, 2, 4, 2), ("yh", "z", "c", "x", "yl"))
    seq, head = ("yh", "z", "c"), ("x", "yl")
    placed = (
        P(seq, head),
        P(seq, head),
        P(seq, head),
        P(seq, head),
        P(head),
        P(head, None),
        P(seq, head),
        P(),
        P(seq, head),
        P(seq, head),
        P(seq, head),
        P(seq, head),
        P(head),
        P(head, None),
    )
    return jax.shard_map(
        local, mesh=fine, in_specs=placed, out_specs=P(seq, head), check_vma=False
    )
```

```python
import jax
import jax.numpy as jnp
from jax import lax
from jax.experimental import pallas as pl
from jax.experimental.pallas import tpu as pltpu
from jax.sharding import Mesh
from jax.sharding import PartitionSpec as P

DH = 128
BLK = 256
TOK = 512
HC = 3
HW = HC * DH
NCHIP = 16
SUB = DH // NCHIP
PIECE = 32
WIDTH = 384
NHEAD = 8
STEPS = 4
KSTEP = 2 * WIDTH
SWAP = [(0, 1), (1, 0)]
VMEM = 16 * 1024 * 1024
F32 = jnp.float32
BF16 = jnp.bfloat16


def silu(u):
    return u / (1.0 + jnp.exp(-u))


def whole(shape):
    return pl.BlockSpec(shape, lambda *_: (0,) * len(shape))


def span(index, size):
    return pl.ds(pl.multiple_of(index * size, DH), size)


def call(kernel, name, place, args, outs, grid=(1,), in_specs=None, out_specs=None, scratch=(), flops=0):
    return pl.pallas_call(
        kernel,
        out_shape=outs,
        grid_spec=pltpu.PrefetchScalarGridSpec(
            num_scalar_prefetch=1,
            grid=grid,
            in_specs=in_specs or [whole(a.shape) for a in args],
            out_specs=out_specs or [whole(o.shape) for o in outs],
            scratch_shapes=scratch,
        ),
        compiler_params=pltpu.CompilerParams(vmem_limit_bytes=VMEM),
        cost_estimate=pl.CostEstimate(flops=flops, bytes_accessed=0, transcendentals=0),
        name=name,
    )(place, *args)


def struct(shape, dtype):
    return jax.ShapeDtypeStruct(shape, dtype)


def in_hbm(a):
    return pltpu.with_memory_space_constraint(a, pltpu.HBM)


def sum_decays(core, mine_ref, yours_ref, cum_ref, across_ref, rows):
    rows[...] = jnp.zeros_like(rows)
    rows[: 4 * HC, span(core, BLK)] = mine_ref[...]
    rows[: 4 * HC, span(1 - core, BLK)] = yours_ref[...]
    before = lax.broadcasted_iota(jnp.int32, (TOK, TOK), 0)
    after = lax.broadcasted_iota(jnp.int32, (TOK, TOK), 1)
    upper = (before <= after).astype(F32)
    sums = jnp.dot(rows[...], upper, preferred_element_type=F32, precision=lax.Precision.HIGHEST)
    first = jnp.where(core == 0, sums[0:HC], sums[HC : 2 * HC])
    second = jnp.where(core == 0, sums[2 * HC : 3 * HC], sums[3 * HC : 4 * HC])
    across = jnp.concatenate([first, second, jnp.zeros((2, TOK), F32)], axis=0)
    across_ref[...] = across
    cum_ref[...] = jnp.concatenate([across, jnp.zeros((DH - 8, TOK), F32)], axis=0).T


def make_pieces(ks, vs, cum_ref, layer, pieces_ref):
    states = []
    decays = jnp.zeros((SUB, DH), F32)
    slot = lax.broadcasted_iota(jnp.int32, (SUB, DH), 0)
    for h in range(HC):
        cols = slice(h * DH, (h + 1) * DH)
        lane = layer * HC + h
        ch = cum_ref[:, lane : lane + 1]
        last = ch[TOK - 1 : TOK]
        kt = (ks[:, cols].astype(F32) * jnp.exp(last - ch)).astype(BF16)
        state = lax.dot_general(kt, vs[:, cols], (((0,), (0,)), ((), ())), preferred_element_type=F32)
        states.append(state.reshape(NCHIP, SUB, DH))
        total = jnp.exp(last)
        high = total.astype(BF16).astype(F32)
        decays = jnp.where(slot == h, high, decays)
        decays = jnp.where(slot == HC + h, total - high, decays)
    states.append(jnp.broadcast_to(decays[None], (NCHIP, SUB, DH)))
    pieces_ref[...] = jnp.concatenate(states, axis=1).astype(BF16)


def make_intra(qs, ks, vs, cum_ref, across_ref, layer, intra_ref):
    lower = lax.broadcasted_iota(jnp.int32, (BLK, BLK), 0) >= lax.broadcasted_iota(
        jnp.int32, (BLK, BLK), 1
    )
    for h in range(HC):
        cols = slice(h * DH, (h + 1) * DH)
        lane = layer * HC + h
        for i in range(2):
            rows = slice(i * BLK, (i + 1) * BLK)
            total = None
            for j in range(i + 1):
                keys = slice(j * BLK, (j + 1) * BLK)
                scores = lax.dot_general(
                    qs[rows, cols], ks[keys, cols], (((1,), (1,)), ((), ())),
                    preferred_element_type=F32,
                )
                spread = cum_ref[rows, lane : lane + 1] - across_ref[lane : lane + 1, keys]
                if i == j:
                    factor = jnp.where(lower, jnp.exp(jnp.where(lower, spread, 0.0)), 0.0)
                else:
                    factor = jnp.exp(spread)
                weights = (scores * factor).astype(BF16)
                part = jnp.dot(weights, vs[keys, cols], preferred_element_type=F32)
                total = part if total is None else total + part
            intra_ref[rows, cols] = total


def both_cores(core, mine_ref, yours_ref, out):
    out[span(core, BLK), :] = silu(mine_ref[:, span(core, HW)].astype(F32)).astype(BF16)
    out[span(1 - core, BLK), :] = silu(yours_ref[:, span(core, HW)].astype(F32)).astype(BF16)


def first_state_kernel(
    place, k_ref, other_k_ref, v_ref, other_v_ref, decay_ref, other_decay_ref,
    pieces_ref, ks, vs, cum_ref, across_ref, rows,
):
    core = place[0]
    both_cores(core, k_ref, other_k_ref, ks)
    both_cores(core, v_ref, other_v_ref, vs)
    sum_decays(core, decay_ref, other_decay_ref, cum_ref, across_ref, rows)
    make_pieces(ks, vs, cum_ref, 0, pieces_ref)


HEADS_OUT = pltpu.HBM((TOK, HW), BF16)
INTRA_OUT = pltpu.HBM((TOK, HW), F32)
PIECES_OUT = struct((NCHIP, PIECE, DH), BF16)


def first_state(place, *args):
    outs = (PIECES_OUT, HEADS_OUT, HEADS_OUT, struct((TOK, DH), F32), struct((8, TOK), F32))
    scratch = (pltpu.VMEM((16, TOK), F32),)
    return call(first_state_kernel, "first_state", place, args, outs, scratch=scratch)


def first_intra_kernel(
    place, q_ref, other_ref, ks, vs, cum_ref, across_ref, intra_ref, qs
):
    core = place[0]
    both_cores(core, q_ref, other_ref, qs)
    make_intra(qs, ks, vs, cum_ref, across_ref, 0, intra_ref)


def first_intra(place, q, other, ks, vs, cum, across):
    args = (q, other, in_hbm(ks), in_hbm(vs), cum, across)
    return call(first_intra_kernel, "first_intra", place, args, (INTRA_OUT, HEADS_OUT))


def project_step(h_ref, w_ref, gain_ref, acc, square, rows):
    step = pl.program_id(0)
    parts = []
    total = None
    for i in range(2):
        wide = h_ref[i].astype(F32)
        parts.append((wide * gain_ref[i]).astype(BF16))
        for n in range(WIDTH // DH):
            tile = wide[:, n * DH : (n + 1) * DH]
            total = tile * tile if total is None else total + tile * tile
    part = jnp.concatenate(parts, axis=1)

    term = jnp.dot(part, w_ref[0], preferred_element_type=F32)

    @pl.when(step == 0)
    def _():
        square[rows, :] = total
        acc[rows, :] = term

    @pl.when(step > 0)
    def _():
        square[rows, :] += total
        acc[rows, :] += term


def row_scale(square):
    mean = jnp.sum(square, axis=-1, keepdims=True) / (NHEAD * WIDTH)
    return lax.rsqrt(mean + 1e-06)


def chunk_at(i, place):
    half = STEPS // 2
    return jnp.where(i < half, place[1] * half + i, (1 - place[1]) * half + i - half), 0, 0


def projection_specs(width):
    half = STEPS // 2
    return (
        pl.BlockSpec((2, BLK, WIDTH), chunk_at),
        pl.BlockSpec((1, KSTEP, width), lambda i, _: (i // half, i % half, 0)),
        pl.BlockSpec((2, 1, WIDTH), chunk_at),
    )


def own_kv_kernel(place, h_ref, w_ref, gain_ref, out_ref, acc, square):
    project_step(h_ref, w_ref, gain_ref, acc, square, slice(0, BLK))

    @pl.when(pl.program_id(0) == STEPS - 1)
    def _():
        out_ref[...] = silu(acc[...] * row_scale(square[...])).astype(BF16)


def own_kv(place, h, w, gain):
    hs, ws, gs = projection_specs(2 * HW)
    return call(
        own_kv_kernel, "own_kv", place, (h, in_hbm(w), gain),
        (struct((BLK, 2 * HW), BF16),),
        grid=(STEPS,), in_specs=[hs, ws, gs],
        scratch=(pltpu.VMEM((BLK, 2 * HW), F32), pltpu.VMEM((BLK, DH), F32)),
        flops=2 * BLK * 2 * HW * NHEAD * WIDTH,
    )[0]


def second_state_kernel(
    place, h_ref, w_ref, gain_ref, own_ref, cum_ref, pieces_ref, ks, vs, acc, square
):
    core = place[0]
    project_step(h_ref, w_ref, gain_ref, acc, square, slice(0, BLK))

    @pl.when(pl.program_id(0) == STEPS - 1)
    def _():
        scale = row_scale(square[...])
        for n, dst in enumerate((ks, vs)):
            cols = slice(n * HW, (n + 1) * HW)
            dst[span(core, BLK), :] = own_ref[:, cols]
            dst[span(1 - core, BLK), :] = silu(acc[:, cols] * scale).astype(BF16)
        make_pieces(ks, vs, cum_ref, 1, pieces_ref)


def second_state(place, h, w, gain, own, cum):
    hs, ws, gs = projection_specs(2 * HW)
    return call(
        second_state_kernel, "second_state", place,
        (h, in_hbm(w), gain, own, cum),
        (PIECES_OUT, HEADS_OUT, HEADS_OUT),
        grid=(STEPS,), in_specs=[hs, ws, gs, whole(own.shape), whole(cum.shape)],
        scratch=(pltpu.VMEM((BLK, 2 * HW), F32), pltpu.VMEM((BLK, DH), F32)),
        flops=2 * BLK * 2 * HW * NHEAD * WIDTH,
    )


def second_intra_kernel(
    place, mine_ref, yours_ref, w_ref, gain_ref, ks, vs, cum_ref, across_ref,
    intra_ref, qs, acc, square,
):
    core = place[0]
    for n, src in enumerate((mine_ref, yours_ref)):
        rows = slice(n * BLK, (n + 1) * BLK)
        project_step(src, w_ref, gain_ref, acc, square, rows)

    @pl.when(pl.program_id(0) == STEPS - 1)
    def _():
        act = silu(acc[...] * row_scale(square[...])).astype(BF16)
        qs[span(core, BLK), :] = act[:BLK]
        qs[span(1 - core, BLK), :] = act[BLK:]
        make_intra(qs, ks, vs, cum_ref, across_ref, 1, intra_ref)


def second_intra(place, mine, yours, w, gain, ks, vs, cum, across):
    hs, ws, gs = projection_specs(HW)
    return call(
        second_intra_kernel, "second_intra", place,
        (mine, yours, in_hbm(w), gain, in_hbm(ks), in_hbm(vs), cum, across),
        (INTRA_OUT, HEADS_OUT),
        grid=(STEPS,),
        in_specs=[hs, hs, ws, gs] + [whole(a.shape) for a in (ks, vs, cum, across)],
        scratch=(pltpu.VMEM((TOK, HW), F32), pltpu.VMEM((TOK, DH), F32)),
    )


def scan_kernel(place, in_ref, out_ref):
    states = [jnp.zeros((SUB, DH), F32) for _ in range(HC)]
    empty = jnp.zeros((PIECE - HC * SUB, DH), F32)
    for p in range(NCHIP):
        piece = in_ref[p].astype(F32)
        out_ref[p] = jnp.concatenate(states + [empty], axis=0).astype(BF16)
        decays = piece[HC * SUB :]
        for h in range(HC):
            decay = decays[h : h + 1] + decays[HC + h : HC + h + 1]
            states[h] = states[h] * decay + piece[h * SUB : (h + 1) * SUB]


def scan(place, pieces):
    return call(scan_kernel, "scan", place, (pieces,), (PIECES_OUT,))[0]


def finish_kernel(
    layer, place, pieces_ref, intra_ref, cum_ref, qs_ref, gain_ref, mine_ref, yours_ref, out
):
    core = place[0]
    pieces = pieces_ref[...].astype(F32)
    for h in range(HC):
        cols = slice(h * DH, (h + 1) * DH)
        lane = layer * HC + h
        state = pieces[:, h * SUB : (h + 1) * SUB].reshape(DH, DH).astype(BF16)
        carried = jnp.dot(qs_ref[:, cols], state, preferred_element_type=F32)
        att = intra_ref[:, cols] + carried * jnp.exp(cum_ref[:, lane : lane + 1])
        square = jnp.mean(att * att, axis=-1, keepdims=True)
        gain = gain_ref[pl.ds(core * HC + h, 1), :]
        out[:, cols] = (att * lax.rsqrt(square + 1e-06) * gain).astype(BF16)
    mine_ref[...] = out[span(core, BLK), :]
    yours_ref[...] = out[span(1 - core, BLK), :]


def finish(place, layer, pieces, intra, cum, qs, gain):
    return call(
        lambda *refs: finish_kernel(layer, *refs), "finish", place,
        (pieces, in_hbm(intra), cum, in_hbm(qs), gain),
        (struct((BLK, HW), BF16),) * 2, scratch=(pltpu.VMEM((TOK, HW), BF16),), flops=0,
    )


def project_kernel(place, mine_ref, yours_ref, w_ref, out_ref, rows):
    core = place[0]

    @pl.when(pl.program_id(0) == 0)
    def _():
        rows[:, span(core, HW)] = mine_ref[...]
        rows[:, span(1 - core, HW)] = yours_ref[...]

    term = jnp.dot(rows[...], w_ref[...], preferred_element_type=F32).astype(BF16)
    out_ref[0] = term[:, :WIDTH]
    out_ref[1] = term[:, WIDTH:]


def project(place, mine, yours, w):
    return call(
        project_kernel, "project", place, (mine, yours, in_hbm(w)),
        (struct((NHEAD, BLK, WIDTH), BF16),),
        grid=(STEPS,),
        in_specs=[
            whole(mine.shape), whole(yours.shape),
            pl.BlockSpec((2 * HW, KSTEP), lambda i, _: (0, i)),
        ],
        out_specs=[pl.BlockSpec((2, BLK, WIDTH), lambda i, _: (i, 0, 0))],
        scratch=(pltpu.VMEM((BLK, 2 * HW), BF16),),
        flops=2 * BLK * 2 * HW * NHEAD * WIDTH,
    )[0]


def exchange(parts, axes):
    return lax.all_to_all(parts, axes, 0, 0)


def after(value, *others):
    return lax.optimization_barrier((value, *others))[0]


def rest(place, layer, before, intra, cum, qs, gain, w):
    mine, yours = finish(place, layer, before, intra, cum, qs, gain.reshape(2 * HC, DH))
    yours = lax.ppermute(yours, "c", SWAP)
    terms = exchange(project(place, mine, yours, w), ("x", "yl"))
    return jnp.sum(terms.astype(F32), axis=0)


def local(
    q1, k1, v1, decay1, gain_out1, wo1, stream_in, gain_in2, wq2, wk2, wv2, decay2, gain_out2, wo2
):
    core = lax.axis_index("c")
    place = jnp.stack([core, lax.axis_index("yh")]).astype(jnp.int32)

    def swapped(*arrays):
        return [lax.ppermute(a, "c", SWAP) for a in arrays]

    decays = jnp.concatenate([decay1.T, decay2.T], axis=0)
    other_k, other_v, other_decays = swapped(k1, v1, decays)
    pieces, ks, vs, cum, across = first_state(
        place, in_hbm(k1), other_k, in_hbm(v1), other_v, decays, other_decays
    )

    *weights, q1, _ = lax.optimization_barrier((wk2, wv2, wq2, q1, pieces))
    other_q, = swapped(q1)
    own_w = jnp.concatenate([lax.dynamic_slice_in_dim(w, core * HW, HW, axis=1) for w in weights], axis=1)
    send_w = [lax.dynamic_slice_in_dim(w, (1 - core) * HW, HW, axis=1) for w in weights]
    other_w, = swapped(jnp.concatenate(send_w, axis=1))
    first = jnp.where(core == 0, own_w, other_w)
    second = jnp.where(core == 0, other_w, own_w)
    near = jnp.concatenate([first, second], axis=0)
    far = lax.ppermute(near, "yh", SWAP)

    sums = after(exchange(pieces, ("yh", "z")), near, other_q)
    far_late = after(far, sums)
    before = exchange(scan(place, sums), ("yh", "z"))

    def gather(cols):
        both = jnp.concatenate([near[None, :, cols], far_late[None, :, cols]], axis=0)
        return both, lambda rows: lax.all_gather(rows, "z", axis=1, tiled=True)

    rows_kv, gather_kv = gather(slice(0, 2 * HW))
    rows_q, gather_q = gather(slice(2 * HW, 3 * HW))
    ks, rows_kv, rows_q = lax.optimization_barrier((ks, rows_kv, rows_q))
    wkv = gather_kv(rows_kv)
    intra, qs = first_intra(place, q1, other_q, ks, vs, cum, across)
    first_share = rest(place, 0, before, intra, cum, qs, gain_out1, wo1)
    stream = (stream_in.astype(F32) + first_share).astype(BF16)
    wq = gather_q(after(rows_q, stream))

    mine = exchange(jnp.broadcast_to(stream[None], (NHEAD, BLK, WIDTH)), ("x", "yl"))
    yours = lax.ppermute(mine, "c", SWAP)
    gain = gain_in2.reshape(NHEAD, 1, WIDTH)
    own = own_kv(place, mine, wkv, gain)
    pieces, ks, vs = second_state(place, yours, wkv, gain, own, cum)
    sums = exchange(pieces, ("yh", "z"))
    before = exchange(scan(place, sums), ("yh", "z"))
    intra, qs = second_intra(place, mine, yours, wq, gain, ks, vs, cum, across)
    second_share = rest(place, 1, before, intra, cum, qs, gain_out2, wo2)
    return (stream.astype(F32) + second_share).astype(BF16)


def solution(mesh):
    fine = Mesh(mesh.devices.reshape(2, 8, 2, 4, 2), ("yh", "z", "c", "x", "yl"))
    seq, head = ("yh", "z", "c"), ("x", "yl")
    both = P(seq, head)
    placed = (
        both, both, both, both, P(head), P(head, None), both, P(),
        both, both, both, both, P(head), P(head, None),
    )
    return jax.shard_map(local, mesh=fine, in_specs=placed, out_specs=both, check_vma=False)
```

```python
import jax
import jax.numpy as jnp
from jax import lax
from jax.experimental import pallas as pl
from jax.experimental.pallas import tpu as pltpu
from jax.sharding import Mesh
from jax.sharding import PartitionSpec as P

DH = 128
BLK = 256
TOK = 512
HC = 3
HW = HC * DH
NCHIP = 16
SUB = DH // NCHIP
PIECE = 32
WIDTH = 384
NHEAD = 8
STEPS = 4
KSTEP = 2 * WIDTH
SWAP = [(0, 1), (1, 0)]
VMEM = 16 * 1024 * 1024
F32 = jnp.float32
BF16 = jnp.bfloat16


def silu(u):
    return u / (1.0 + jnp.exp(-u))


def whole(shape):
    return pl.BlockSpec(shape, lambda *_: (0,) * len(shape))


def span(index, size):
    return pl.ds(pl.multiple_of(index * size, DH), size)


def call(kernel, name, place, args, outs, grid=(1,), in_specs=None, out_specs=None, scratch=(), flops=0):
    return pl.pallas_call(
        kernel,
        out_shape=outs,
        grid_spec=pltpu.PrefetchScalarGridSpec(
            num_scalar_prefetch=1,
            grid=grid,
            in_specs=in_specs or [whole(a.shape) for a in args],
            out_specs=out_specs or [whole(o.shape) for o in outs],
            scratch_shapes=scratch,
        ),
        compiler_params=pltpu.CompilerParams(vmem_limit_bytes=VMEM),
        cost_estimate=pl.CostEstimate(flops=flops, bytes_accessed=0, transcendentals=0),
        name=name,
    )(place, *args)


def struct(shape, dtype):
    return jax.ShapeDtypeStruct(shape, dtype)


def in_hbm(a):
    return pltpu.with_memory_space_constraint(a, pltpu.HBM)


def sum_decays(core, mine_ref, yours_ref, cum_ref, across_ref, rows):
    rows[...] = jnp.zeros_like(rows)
    rows[: 4 * HC, span(core, BLK)] = mine_ref[...]
    rows[: 4 * HC, span(1 - core, BLK)] = yours_ref[...]
    before = lax.broadcasted_iota(jnp.int32, (TOK, TOK), 0)
    after = lax.broadcasted_iota(jnp.int32, (TOK, TOK), 1)
    upper = (before <= after).astype(F32)
    sums = jnp.dot(rows[...], upper, preferred_element_type=F32, precision=lax.Precision.HIGHEST)
    first = jnp.where(core == 0, sums[0:HC], sums[HC : 2 * HC])
    second = jnp.where(core == 0, sums[2 * HC : 3 * HC], sums[3 * HC : 4 * HC])
    across = jnp.concatenate([first, second, jnp.zeros((2, TOK), F32)], axis=0)
    across_ref[...] = across
    cum_ref[...] = jnp.concatenate([across, jnp.zeros((DH - 8, TOK), F32)], axis=0).T


def make_pieces(ks, vs, cum_ref, layer, pieces_ref):
    states = []
    decays = jnp.zeros((SUB, DH), F32)
    slot = lax.broadcasted_iota(jnp.int32, (SUB, DH), 0)
    for h in range(HC):
        cols = slice(h * DH, (h + 1) * DH)
        lane = layer * HC + h
        ch = cum_ref[:, lane : lane + 1]
        last = ch[TOK - 1 : TOK]
        kt = (ks[:, cols].astype(F32) * jnp.exp(last - ch)).astype(BF16)
        state = lax.dot_general(kt, vs[:, cols], (((0,), (0,)), ((), ())), preferred_element_type=F32)
        states.append(state.reshape(NCHIP, SUB, DH))
        total = jnp.exp(last)
        high = total.astype(BF16).astype(F32)
        decays = jnp.where(slot == h, high, decays)
        decays = jnp.where(slot == HC + h, total - high, decays)
    states.append(jnp.broadcast_to(decays[None], (NCHIP, SUB, DH)))
    pieces_ref[...] = jnp.concatenate(states, axis=1).astype(BF16)


def make_intra(qs, ks, vs, cum_ref, across_ref, layer, intra_ref):
    lower = lax.broadcasted_iota(jnp.int32, (BLK, BLK), 0) >= lax.broadcasted_iota(
        jnp.int32, (BLK, BLK), 1
    )
    for h in range(HC):
        cols = slice(h * DH, (h + 1) * DH)
        lane = layer * HC + h
        for i in range(2):
            rows = slice(i * BLK, (i + 1) * BLK)
            total = None
            for j in range(i + 1):
                keys = slice(j * BLK, (j + 1) * BLK)
                scores = lax.dot_general(
                    qs[rows, cols], ks[keys, cols], (((1,), (1,)), ((), ())),
                    preferred_element_type=F32,
                )
                spread = cum_ref[rows, lane : lane + 1] - across_ref[lane : lane + 1, keys]
                if i == j:
                    factor = jnp.where(lower, jnp.exp(jnp.where(lower, spread, 0.0)), 0.0)
                else:
                    factor = jnp.exp(spread)
                weights = (scores * factor).astype(BF16)
                part = jnp.dot(weights, vs[keys, cols], preferred_element_type=F32)
                total = part if total is None else total + part
            intra_ref[rows, cols] = total


def both_cores(core, mine_ref, yours_ref, out):
    out[span(core, BLK), :] = silu(mine_ref[:, span(core, HW)].astype(F32)).astype(BF16)
    out[span(1 - core, BLK), :] = silu(yours_ref[:, span(core, HW)].astype(F32)).astype(BF16)


def first_state_kernel(
    place, k_ref, other_k_ref, v_ref, other_v_ref, decay_ref, other_decay_ref,
    pieces_ref, ks, vs, cum_ref, across_ref, rows,
):
    core = place[0]
    both_cores(core, k_ref, other_k_ref, ks)
    both_cores(core, v_ref, other_v_ref, vs)
    sum_decays(core, decay_ref, other_decay_ref, cum_ref, across_ref, rows)
    make_pieces(ks, vs, cum_ref, 0, pieces_ref)


IN_VMEM = pl.BlockSpec(memory_space=pltpu.VMEM)
ANY = pl.BlockSpec(memory_space=pl.ANY)
HEADS_OUT = pltpu.HBM((TOK, HW), BF16)
QUERY_OUT = struct((TOK, HW), BF16)
INTRA_OUT = struct((TOK, HW), F32)
WO_OUT = pltpu.VMEM((2 * HW, NHEAD * WIDTH), BF16)
WKV_OUT = pltpu.VMEM((2, NHEAD * WIDTH // 2, 2 * HW), BF16)
PIECES_OUT = struct((NCHIP, PIECE, DH), BF16)


def first_state(place, *args):
    outs = (PIECES_OUT, HEADS_OUT, HEADS_OUT, struct((TOK, DH), F32), struct((8, TOK), F32))
    scratch = (pltpu.VMEM((16, TOK), F32),)
    return call(first_state_kernel, "first_state", place, args, outs, scratch=scratch)


def first_intra_kernel(
    place, q_ref, other_ref, ks, vs, cum_ref, across_ref, intra_ref, qs
):
    core = place[0]
    both_cores(core, q_ref, other_ref, qs)
    make_intra(qs, ks, vs, cum_ref, across_ref, 0, intra_ref)


def first_intra(place, q, other, ks, vs, cum, across):
    args = (q, other, in_hbm(ks), in_hbm(vs), cum, across)
    return call(first_intra_kernel, "first_intra", place, args, (INTRA_OUT, QUERY_OUT))


def project_step(h_ref, w, gain_ref, acc, square, rows):
    step = pl.program_id(0)
    parts = []
    total = None
    for i in range(2):
        wide = h_ref[i].astype(F32)
        parts.append((wide * gain_ref[i]).astype(BF16))
        for n in range(WIDTH // DH):
            tile = wide[:, n * DH : (n + 1) * DH]
            total = tile * tile if total is None else total + tile * tile
    part = jnp.concatenate(parts, axis=1)

    term = jnp.dot(part, w, preferred_element_type=F32)

    @pl.when(step == 0)
    def _():
        square[rows, :] = total
        acc[rows, :] = term

    @pl.when(step > 0)
    def _():
        square[rows, :] += total
        acc[rows, :] += term


def row_scale(square):
    mean = jnp.sum(square, axis=-1, keepdims=True) / (NHEAD * WIDTH)
    return lax.rsqrt(mean + 1e-06)


def chunk_at(i, place):
    half = STEPS // 2
    return jnp.where(i < half, place[1] * half + i, (1 - place[1]) * half + i - half), 0, 0


def projection_specs(width):
    half = STEPS // 2
    return (
        pl.BlockSpec((2, BLK, WIDTH), chunk_at),
        pl.BlockSpec((1, KSTEP, width), lambda i, _: (i // half, i % half, 0)),
        pl.BlockSpec((2, 1, WIDTH), chunk_at),
    )


def weight_rows(w_ref):
    half = STEPS // 2
    step = pl.program_id(0)
    return w_ref.at[step // half, pl.ds(pl.multiple_of(step % half * KSTEP, KSTEP), KSTEP), :]


def own_kv_kernel(place, h_ref, w_ref, gain_ref, out_ref, held, acc, square, sems):
    step = pl.program_id(0)
    half = STEPS // 2

    def fetch(n):
        rows = pl.ds(n % half * KSTEP, KSTEP)
        return pltpu.make_async_copy(
            w_ref.at[n // half, rows, :], held.at[n // half, rows, :], sems.at[n]
        )

    @pl.when(step == 0)
    def _():
        for n in range(STEPS):
            fetch(n).start()

    for n in range(STEPS):

        @pl.when(step == n)
        def _(n=n):
            fetch(n).wait()

    project_step(h_ref, weight_rows(held)[...], gain_ref, acc, square, slice(0, BLK))

    @pl.when(step == STEPS - 1)
    def _():
        out_ref[...] = silu(acc[...] * row_scale(square[...])).astype(BF16)


def own_kv(place, h, w, gain):
    hs, _, gs = projection_specs(2 * HW)
    return call(
        own_kv_kernel, "own_kv", place, (h, in_hbm(w), gain),
        (struct((BLK, 2 * HW), BF16), WKV_OUT),
        grid=(STEPS,), in_specs=[hs, ANY, gs], out_specs=[whole((BLK, 2 * HW)), IN_VMEM],
        scratch=(
            pltpu.VMEM((BLK, 2 * HW), F32), pltpu.VMEM((BLK, DH), F32),
            pltpu.SemaphoreType.DMA((STEPS,)),
        ),
    )


def second_state_kernel(
    place, h_ref, w_ref, gain_ref, own_ref, cum_ref, pieces_ref, ks, vs, acc, square
):
    core = place[0]
    project_step(h_ref, weight_rows(w_ref)[...], gain_ref, acc, square, slice(0, BLK))

    @pl.when(pl.program_id(0) == STEPS - 1)
    def _():
        scale = row_scale(square[...])
        for n, dst in enumerate((ks, vs)):
            cols = slice(n * HW, (n + 1) * HW)
            dst[span(core, BLK), :] = own_ref[:, cols]
            dst[span(1 - core, BLK), :] = silu(acc[:, cols] * scale).astype(BF16)
        make_pieces(ks, vs, cum_ref, 1, pieces_ref)


def second_state(place, h, w, gain, own, cum):
    hs, _, gs = projection_specs(2 * HW)
    return call(
        second_state_kernel, "second_state", place, (h, w, gain, own, cum),
        (PIECES_OUT, HEADS_OUT, HEADS_OUT),
        grid=(STEPS,), in_specs=[hs, IN_VMEM, gs, whole(own.shape), whole(cum.shape)],
        scratch=(pltpu.VMEM((BLK, 2 * HW), F32), pltpu.VMEM((BLK, DH), F32)),
    )


def second_intra_kernel(
    place, mine_ref, yours_ref, w_ref, gain_ref, ks, vs, cum_ref, across_ref,
    intra_ref, qs, acc, square,
):
    core = place[0]
    for n, src in enumerate((mine_ref, yours_ref)):
        rows = slice(n * BLK, (n + 1) * BLK)
        project_step(src, w_ref[0], gain_ref, acc, square, rows)

    @pl.when(pl.program_id(0) == STEPS - 1)
    def _():
        act = silu(acc[...] * row_scale(square[...])).astype(BF16)
        qs[span(core, BLK), :] = act[:BLK]
        qs[span(1 - core, BLK), :] = act[BLK:]
        make_intra(qs, ks, vs, cum_ref, across_ref, 1, intra_ref)


def second_intra(place, mine, yours, w, gain, ks, vs, cum, across):
    hs, ws, gs = projection_specs(HW)
    return call(
        second_intra_kernel, "second_intra", place,
        (mine, yours, in_hbm(w), gain, in_hbm(ks), in_hbm(vs), cum, across),
        (pltpu.HBM((TOK, HW), F32), HEADS_OUT),
        grid=(STEPS,),
        in_specs=[hs, hs, ws, gs] + [whole(a.shape) for a in (ks, vs, cum, across)],
        scratch=(pltpu.VMEM((TOK, HW), F32), pltpu.VMEM((TOK, DH), F32)),
    )


def pack_kernel(place, own_ref, other_ref, far_ref, far_other_ref, kv_ref, q_ref):
    core = place[0]
    rows = own_ref.shape[0]
    for n, pair in enumerate(((own_ref, other_ref), (far_ref, far_other_ref))):
        for src, owner in zip(pair, (core, 1 - core)):
            at = pl.ds(pl.multiple_of(owner * rows, rows), rows)
            for i in range(2):
                kv_ref[n, at, i * HW : (i + 1) * HW] = src[:, span(2 * i + core, HW)]
            q_ref[n, at, :] = src[:, span(4 + core, HW)]


def pack(place, *args):
    rows = 2 * args[0].shape[0]
    outs = (struct((2, rows, 2 * HW), BF16), struct((2, rows, HW), BF16))
    return call(pack_kernel, "pack", place, args, outs)


def scan_kernel(place, in_ref, out_ref):
    states = [jnp.zeros((SUB, DH), F32) for _ in range(HC)]
    empty = jnp.zeros((PIECE - HC * SUB, DH), F32)
    for p in range(NCHIP):
        piece = in_ref[p].astype(F32)
        out_ref[p] = jnp.concatenate(states + [empty], axis=0).astype(BF16)
        decays = piece[HC * SUB :]
        for h in range(HC):
            decay = decays[h : h + 1] + decays[HC + h : HC + h + 1]
            states[h] = states[h] * decay + piece[h * SUB : (h + 1) * SUB]


def scan(place, pieces):
    return call(scan_kernel, "scan", place, (pieces,), (PIECES_OUT,))[0]


def finish_kernel(
    layer, place, pieces_ref, intra_ref, cum_ref, qs_ref, gain_ref, wo_ref,
    mine_ref, yours_ref, held, out, sem,
):
    core = place[0]
    fetch = pltpu.make_async_copy(wo_ref, held, sem)
    fetch.start()
    pieces = pieces_ref[...].astype(F32)
    for h in range(HC):
        cols = slice(h * DH, (h + 1) * DH)
        lane = layer * HC + h
        state = pieces[:, h * SUB : (h + 1) * SUB].reshape(DH, DH).astype(BF16)
        carried = jnp.dot(qs_ref[:, cols], state, preferred_element_type=F32)
        att = intra_ref[:, cols] + carried * jnp.exp(cum_ref[:, lane : lane + 1])
        square = jnp.mean(att * att, axis=-1, keepdims=True)
        gain = gain_ref[pl.ds(core * HC + h, 1), :]
        out[:, cols] = (att * lax.rsqrt(square + 1e-06) * gain).astype(BF16)
    mine_ref[...] = out[span(core, BLK), :]
    yours_ref[...] = out[span(1 - core, BLK), :]
    fetch.wait()


def finish(place, layer, pieces, intra, cum, qs, gain, wo):
    if layer:
        intra, qs = in_hbm(intra), in_hbm(qs)
    args = (pieces, intra, cum, qs, gain)
    return call(
        lambda *refs: finish_kernel(layer, *refs), "finish", place, (*args, in_hbm(wo)),
        (struct((BLK, HW), BF16), struct((BLK, HW), BF16), WO_OUT),
        in_specs=[whole(a.shape) for a in args] + [ANY],
        out_specs=[whole((BLK, HW)), whole((BLK, HW)), IN_VMEM],
        scratch=(pltpu.VMEM((TOK, HW), BF16), pltpu.SemaphoreType.DMA),
    )


def project_kernel(place, mine_ref, yours_ref, w_ref, out_ref, rows):
    core = place[0]

    @pl.when(pl.program_id(0) == 0)
    def _():
        rows[:, span(core, HW)] = mine_ref[...]
        rows[:, span(1 - core, HW)] = yours_ref[...]

    cols = span(pl.program_id(0), KSTEP)
    term = jnp.dot(rows[...], w_ref[:, cols], preferred_element_type=F32).astype(BF16)
    out_ref[0] = term[:, :WIDTH]
    out_ref[1] = term[:, WIDTH:]


def project(place, mine, yours, w):
    return call(
        project_kernel, "project", place, (mine, yours, w),
        (struct((NHEAD, BLK, WIDTH), BF16),),
        grid=(STEPS,),
        in_specs=[
            whole(mine.shape), whole(yours.shape),
            IN_VMEM,
        ],
        out_specs=[pl.BlockSpec((2, BLK, WIDTH), lambda i, _: (i, 0, 0))],
        scratch=(pltpu.VMEM((BLK, 2 * HW), BF16),),
        flops=2 * BLK * 2 * HW * NHEAD * WIDTH,
    )[0]


def exchange(parts, axes):
    return lax.all_to_all(parts, axes, 0, 0)


def after(value, *others):
    return lax.optimization_barrier((value, *others))[0]


def rest(place, layer, before, intra, cum, qs, gain, w):
    mine, yours, w = finish(place, layer, before, intra, cum, qs, gain.reshape(2 * HC, DH), w)
    yours = lax.ppermute(yours, "c", SWAP)
    terms = exchange(project(place, mine, yours, w), ("x", "yl"))
    return jnp.sum(terms.astype(F32), axis=0)


def local(
    q1, k1, v1, decay1, gain_out1, wo1, stream_in, gain_in2, wq2, wk2, wv2, decay2, gain_out2, wo2
):
    core = lax.axis_index("c")
    place = jnp.stack([core, lax.axis_index("yh")]).astype(jnp.int32)

    def swapped(*arrays):
        return [lax.ppermute(a, "c", SWAP) for a in arrays]

    decays = jnp.concatenate([decay1.T, decay2.T], axis=0)
    other_k, other_v, other_decays = swapped(k1, v1, decays)
    pieces, ks, vs, cum, across = first_state(
        place, in_hbm(k1), other_k, in_hbm(v1), other_v, decays, other_decays
    )

    w_cat = jnp.concatenate([wk2, wv2, wq2], axis=1)
    far = lax.ppermute(w_cat, "yh", SWAP)
    other_w, = swapped(w_cat)
    q1 = after(q1, pieces)
    other_q, = swapped(q1)
    sums = after(exchange(pieces, ("yh", "z")), other_q)
    scanned = scan(place, sums)
    far = after(far, scanned)
    far_other, = swapped(far)
    rows_kv, rows_q = pack(place, w_cat, other_w, far, far_other)
    before = exchange(scanned, ("yh", "z"))

    def gather(rows):
        return lax.all_gather(rows, "z", axis=1, tiled=True)

    ks, rows_kv, rows_q = lax.optimization_barrier((ks, rows_kv, rows_q))
    wkv = gather(rows_kv)
    intra, qs = first_intra(place, q1, other_q, ks, vs, cum, across)
    first_share = rest(place, 0, before, intra, cum, qs, gain_out1, wo1)
    stream = (stream_in.astype(F32) + first_share).astype(BF16)
    wq = gather(after(rows_q, stream))

    mine = exchange(jnp.broadcast_to(stream[None], (NHEAD, BLK, WIDTH)), ("x", "yl"))
    yours = lax.ppermute(mine, "c", SWAP)
    gain = gain_in2.reshape(NHEAD, 1, WIDTH)
    own, wkv = own_kv(place, mine, wkv, gain)
    pieces, ks, vs = second_state(place, yours, wkv, gain, own, cum)
    sums = exchange(pieces, ("yh", "z"))
    before = exchange(scan(place, sums), ("yh", "z"))
    intra, qs = second_intra(place, mine, yours, wq, gain, ks, vs, cum, across)
    second_share = rest(place, 1, before, intra, cum, qs, gain_out2, wo2)
    return (stream.astype(F32) + second_share).astype(BF16)


def solution(mesh):
    fine = Mesh(mesh.devices.reshape(2, 8, 2, 4, 2), ("yh", "z", "c", "x", "yl"))
    seq, head = ("yh", "z", "c"), ("x", "yl")
    both = P(seq, head)
    placed = (
        both, both, both, both, P(head), P(head, None), both, P(),
        both, both, both, both, P(head), P(head, None),
    )
    return jax.shard_map(local, mesh=fine, in_specs=placed, out_specs=both, check_vma=False)
```

```python
import jax
import jax.numpy as jnp
from jax import lax
from jax.experimental import pallas as pl
from jax.experimental.pallas import tpu as pltpu
from jax.sharding import Mesh
from jax.sharding import PartitionSpec as P

DH = 128
BLK = 256
TOK = 512
HC = 3
HW = HC * DH
NCHIP = 16
SUB = DH // NCHIP
PIECE = 32
WIDTH = 384
NHEAD = 8
STEPS = 4
KSTEP = 2 * WIDTH
SWAP = [(0, 1), (1, 0)]
VMEM = 16 * 1024 * 1024
F32 = jnp.float32
BF16 = jnp.bfloat16


def silu(u):
    return u / (1.0 + jnp.exp(-u))


def whole(shape):
    return pl.BlockSpec(shape, lambda *_: (0,) * len(shape))


def span(index, size):
    return pl.ds(pl.multiple_of(index * size, DH), size)


def call(kernel, name, place, args, outs, grid=(1,), in_specs=None, out_specs=None, scratch=(), flops=0):
    return pl.pallas_call(
        kernel,
        out_shape=outs,
        grid_spec=pltpu.PrefetchScalarGridSpec(
            num_scalar_prefetch=1,
            grid=grid,
            in_specs=in_specs or [whole(a.shape) for a in args],
            out_specs=out_specs or [whole(o.shape) for o in outs],
            scratch_shapes=scratch,
        ),
        compiler_params=pltpu.CompilerParams(vmem_limit_bytes=VMEM),
        cost_estimate=pl.CostEstimate(flops=flops, bytes_accessed=0, transcendentals=0),
        name=name,
    )(place, *args)


def struct(shape, dtype):
    return jax.ShapeDtypeStruct(shape, dtype)


def in_hbm(a):
    return pltpu.with_memory_space_constraint(a, pltpu.HBM)


def sum_decays(core, mine_ref, yours_ref, cum_ref, across_ref, rows):
    rows[...] = jnp.zeros_like(rows)
    rows[: 4 * HC, span(core, BLK)] = mine_ref[...]
    rows[: 4 * HC, span(1 - core, BLK)] = yours_ref[...]
    before = lax.broadcasted_iota(jnp.int32, (TOK, TOK), 0)
    after = lax.broadcasted_iota(jnp.int32, (TOK, TOK), 1)
    upper = (before <= after).astype(F32)
    sums = jnp.dot(rows[...], upper, preferred_element_type=F32, precision=lax.Precision.HIGHEST)
    first = jnp.where(core == 0, sums[0:HC], sums[HC : 2 * HC])
    second = jnp.where(core == 0, sums[2 * HC : 3 * HC], sums[3 * HC : 4 * HC])
    across = jnp.concatenate([first, second, jnp.zeros((2, TOK), F32)], axis=0)
    across_ref[...] = across
    cum_ref[...] = jnp.concatenate([across, jnp.zeros((DH - 8, TOK), F32)], axis=0).T


def make_pieces(ks, vs, cum_ref, layer, pieces_ref):
    states = []
    decays = jnp.zeros((SUB, DH), F32)
    slot = lax.broadcasted_iota(jnp.int32, (SUB, DH), 0)
    for h in range(HC):
        cols = slice(h * DH, (h + 1) * DH)
        lane = layer * HC + h
        ch = cum_ref[:, lane : lane + 1]
        last = ch[TOK - 1 : TOK]
        kt = (ks[:, cols].astype(F32) * jnp.exp(last - ch)).astype(BF16)
        state = lax.dot_general(kt, vs[:, cols], (((0,), (0,)), ((), ())), preferred_element_type=F32)
        states.append(state.reshape(NCHIP, SUB, DH))
        total = jnp.exp(last)
        high = total.astype(BF16).astype(F32)
        decays = jnp.where(slot == h, high, decays)
        decays = jnp.where(slot == HC + h, total - high, decays)
    states.append(jnp.broadcast_to(decays[None], (NCHIP, SUB, DH)))
    pieces_ref[...] = jnp.concatenate(states, axis=1).astype(BF16)


def make_intra(qs, ks, vs, cum_ref, across_ref, layer, intra_ref):
    lower = lax.broadcasted_iota(jnp.int32, (BLK, BLK), 0) >= lax.broadcasted_iota(
        jnp.int32, (BLK, BLK), 1
    )
    for h in range(HC):
        cols = slice(h * DH, (h + 1) * DH)
        lane = layer * HC + h
        for i in range(2):
            rows = slice(i * BLK, (i + 1) * BLK)
            total = None
            for j in range(i + 1):
                keys = slice(j * BLK, (j + 1) * BLK)
                scores = lax.dot_general(
                    qs[rows, cols], ks[keys, cols], (((1,), (1,)), ((), ())),
                    preferred_element_type=F32,
                )
                spread = cum_ref[rows, lane : lane + 1] - across_ref[lane : lane + 1, keys]
                if i == j:
                    factor = jnp.where(lower, jnp.exp(jnp.where(lower, spread, 0.0)), 0.0)
                else:
                    factor = jnp.exp(spread)
                weights = (scores * factor).astype(BF16)
                part = jnp.dot(weights, vs[keys, cols], preferred_element_type=F32)
                total = part if total is None else total + part
            intra_ref[rows, cols] = total


def both_cores(core, mine_ref, yours_ref, out):
    out[span(core, BLK), :] = silu(mine_ref[...].astype(F32)).astype(BF16)
    out[span(1 - core, BLK), :] = silu(yours_ref[...].astype(F32)).astype(BF16)


HALF = pl.BlockSpec((BLK, HW), lambda _, place: (0, place[0]))


def first_state_kernel(
    place, k_ref, other_k_ref, v_ref, other_v_ref, decay_ref, other_decay_ref,
    pieces_ref, ks, vs, cum_ref, across_ref, rows,
):
    core = place[0]
    both_cores(core, k_ref, other_k_ref, ks)
    both_cores(core, v_ref, other_v_ref, vs)
    sum_decays(core, decay_ref, other_decay_ref, cum_ref, across_ref, rows)
    make_pieces(ks, vs, cum_ref, 0, pieces_ref)


IN_VMEM = pl.BlockSpec(memory_space=pltpu.VMEM)
ANY = pl.BlockSpec(memory_space=pl.ANY)
HEADS_OUT = pltpu.HBM((TOK, HW), BF16)
QUERY_OUT = struct((TOK, HW), BF16)
INTRA_OUT = struct((TOK, HW), F32)
WO_HALF = (2 * HW, NHEAD * WIDTH // 2)
WKV_OUT = pltpu.VMEM((2, NHEAD * WIDTH // 2, 2 * HW), BF16)
PIECES_OUT = struct((NCHIP, PIECE, DH), BF16)


def first_state(place, *args):
    outs = (PIECES_OUT, HEADS_OUT, HEADS_OUT, struct((TOK, DH), F32), struct((8, TOK), F32))
    scratch = (pltpu.VMEM((16, TOK), F32),)
    specs = [HALF] * 4 + [whole(a.shape) for a in args[4:]]
    return call(
        first_state_kernel, "first_state", place, args, outs, in_specs=specs, scratch=scratch
    )


def cut_kernel(place, k_ref, v_ref, q_ref, both_ref, give_ref):
    core = place[0]
    for n, src in enumerate((k_ref, v_ref, q_ref)):
        both_ref[:, n * HW : (n + 1) * HW] = src[:, span(core, HW)]
        give = src[:, span(1 - core, HW)]
        both_ref[:, (n + 3) * HW : (n + 4) * HW] = give
        give_ref[:, n * HW : (n + 1) * HW] = give


def cut(place, *weights):
    rows = weights[0].shape[0]
    outs = (struct((rows, 6 * HW), BF16), struct((rows, 3 * HW), BF16))
    return call(cut_kernel, "cut", place, weights, outs)


def pack_kernel(place, near_ref, near_other_ref, far_ref, far_other_ref, kv_ref, wq_ref):
    core = place[0]
    rows = near_ref.shape[0]
    for n, pair in enumerate(((near_ref, near_other_ref), (far_ref, far_other_ref))):
        for src, owner in zip(pair, (core, 1 - core)):
            at = pl.ds(pl.multiple_of(owner * rows, rows), rows)
            kv_ref[n, at, :] = src[:, : 2 * HW]
            wq_ref[n, at, :] = src[:, 2 * HW : 3 * HW]


def pack(place, *parts):
    rows = 2 * parts[0].shape[0]
    outs = (pltpu.HBM((2, rows, 2 * HW), BF16), pltpu.HBM((2, rows, HW), BF16))
    return call(pack_kernel, "pack", place, parts, outs)


def first_intra_kernel(place, q_ref, other_ref, ks, vs, cum_ref, across_ref, intra_ref, qs):
    both_cores(place[0], q_ref, other_ref, qs)
    make_intra(qs, ks, vs, cum_ref, across_ref, 0, intra_ref)


def first_intra(place, q, other, ks, vs, cum, across):
    args = (q, other, in_hbm(ks), in_hbm(vs), cum, across)
    specs = [HALF] * 2 + [whole(a.shape) for a in args[2:]]
    return call(
        first_intra_kernel, "first_intra", place, args, (INTRA_OUT, QUERY_OUT), in_specs=specs
    )


def project_step(h_ref, w, gain_ref, acc, square, rows):
    step = pl.program_id(0)
    parts = []
    total = None
    for i in range(2):
        wide = h_ref[i].astype(F32)
        parts.append((wide * gain_ref[i]).astype(BF16))
        for n in range(WIDTH // DH):
            tile = wide[:, n * DH : (n + 1) * DH]
            total = tile * tile if total is None else total + tile * tile
    part = jnp.concatenate(parts, axis=1)

    term = jnp.dot(part, w, preferred_element_type=F32)

    @pl.when(step == 0)
    def _():
        square[rows, :] = total
        acc[rows, :] = term

    @pl.when(step > 0)
    def _():
        square[rows, :] += total
        acc[rows, :] += term


def row_scale(square):
    mean = jnp.sum(square, axis=-1, keepdims=True) / (NHEAD * WIDTH)
    return lax.rsqrt(mean + 1e-06)


def chunk_at(i, place):
    half = STEPS // 2
    return jnp.where(i < half, place[1] * half + i, (1 - place[1]) * half + i - half), 0, 0


def projection_specs(width):
    half = STEPS // 2
    return (
        pl.BlockSpec((2, BLK, WIDTH), chunk_at),
        pl.BlockSpec((1, KSTEP, width), lambda i, _: (i // half, i % half, 0)),
        pl.BlockSpec((2, 1, WIDTH), chunk_at),
    )


def weight_rows(w_ref):
    half = STEPS // 2
    step = pl.program_id(0)
    return w_ref.at[step // half, pl.ds(pl.multiple_of(step % half * KSTEP, KSTEP), KSTEP), :]


def own_kv_kernel(place, h_ref, w_ref, gain_ref, out_ref, held, acc, square, sems):
    step = pl.program_id(0)
    half = STEPS // 2

    def fetch(n):
        rows = pl.ds(n % half * KSTEP, KSTEP)
        return pltpu.make_async_copy(
            w_ref.at[n // half, rows, :], held.at[n // half, rows, :], sems.at[n]
        )

    @pl.when(step == 0)
    def _():
        for n in range(STEPS):
            fetch(n).start()

    for n in range(STEPS):

        @pl.when(step == n)
        def _(n=n):
            fetch(n).wait()

    project_step(h_ref, weight_rows(held)[...], gain_ref, acc, square, slice(0, BLK))

    @pl.when(step == STEPS - 1)
    def _():
        out_ref[...] = silu(acc[...] * row_scale(square[...])).astype(BF16)


def own_kv(place, h, w, gain):
    hs, _, gs = projection_specs(2 * HW)
    return call(
        own_kv_kernel, "own_kv", place, (h, in_hbm(w), gain),
        (struct((BLK, 2 * HW), BF16), WKV_OUT),
        grid=(STEPS,), in_specs=[hs, ANY, gs], out_specs=[whole((BLK, 2 * HW)), IN_VMEM],
        scratch=(
            pltpu.VMEM((BLK, 2 * HW), F32), pltpu.VMEM((BLK, DH), F32),
            pltpu.SemaphoreType.DMA((STEPS,)),
        ),
    )


def second_state_kernel(
    place, h_ref, w_ref, gain_ref, own_ref, cum_ref, pieces_ref, ks, vs, acc, square
):
    core = place[0]
    project_step(h_ref, weight_rows(w_ref)[...], gain_ref, acc, square, slice(0, BLK))

    @pl.when(pl.program_id(0) == STEPS - 1)
    def _():
        scale = row_scale(square[...])
        for n, dst in enumerate((ks, vs)):
            cols = slice(n * HW, (n + 1) * HW)
            dst[span(core, BLK), :] = own_ref[:, cols]
            dst[span(1 - core, BLK), :] = silu(acc[:, cols] * scale).astype(BF16)
        make_pieces(ks, vs, cum_ref, 1, pieces_ref)


def second_state(place, h, w, gain, own, cum):
    hs, _, gs = projection_specs(2 * HW)
    return call(
        second_state_kernel, "second_state", place, (h, w, gain, own, cum),
        (PIECES_OUT, HEADS_OUT, HEADS_OUT),
        grid=(STEPS,), in_specs=[hs, IN_VMEM, gs, whole(own.shape), whole(cum.shape)],
        scratch=(pltpu.VMEM((BLK, 2 * HW), F32), pltpu.VMEM((BLK, DH), F32)),
    )


def second_intra_kernel(
    place, mine_ref, yours_ref, w_ref, gain_ref, ks, vs, cum_ref, across_ref,
    intra_ref, qs, acc, square,
):
    core = place[0]
    for n, src in enumerate((mine_ref, yours_ref)):
        rows = slice(n * BLK, (n + 1) * BLK)
        project_step(src, w_ref[0], gain_ref, acc, square, rows)

    @pl.when(pl.program_id(0) == STEPS - 1)
    def _():
        act = silu(acc[...] * row_scale(square[...])).astype(BF16)
        qs[span(core, BLK), :] = act[:BLK]
        qs[span(1 - core, BLK), :] = act[BLK:]
        make_intra(qs, ks, vs, cum_ref, across_ref, 1, intra_ref)


def second_intra(place, mine, yours, w, gain, ks, vs, cum, across):
    hs, ws, gs = projection_specs(HW)
    return call(
        second_intra_kernel, "second_intra", place,
        (mine, yours, in_hbm(w), gain, in_hbm(ks), in_hbm(vs), cum, in_hbm(across)),
        (pltpu.HBM((TOK, HW), F32), HEADS_OUT),
        grid=(STEPS,),
        in_specs=[hs, hs, ws, gs] + [whole(a.shape) for a in (ks, vs, cum, across)],
        scratch=(pltpu.VMEM((TOK, HW), F32), pltpu.VMEM((TOK, DH), F32)),
    )


def scan_kernel(place, in_ref, out_ref):
    states = [jnp.zeros((SUB, DH), F32) for _ in range(HC)]
    empty = jnp.zeros((PIECE - HC * SUB, DH), F32)
    for p in range(NCHIP):
        piece = in_ref[p].astype(F32)
        out_ref[p] = jnp.concatenate(states + [empty], axis=0).astype(BF16)
        decays = piece[HC * SUB :]
        for h in range(HC):
            decay = decays[h : h + 1] + decays[HC + h : HC + h + 1]
            states[h] = states[h] * decay + piece[h * SUB : (h + 1) * SUB]


def scan(place, pieces):
    outs = (pltpu.HBM((NCHIP, PIECE, DH), BF16),)
    return call(scan_kernel, "scan", place, (pieces,), outs)[0]


def finish_kernel(
    layer, place, pieces_ref, intra_ref, cum_ref, qs_ref, gain_ref, wo_ref,
    mine_ref, yours_ref, held, out, sem,
):
    core = place[0]
    fetch = pltpu.make_async_copy(wo_ref.at[:, : WO_HALF[1]], held, sem)
    fetch.start()
    pieces = pieces_ref[...].astype(F32)
    for h in range(HC):
        cols = slice(h * DH, (h + 1) * DH)
        lane = layer * HC + h
        state = pieces[:, h * SUB : (h + 1) * SUB].reshape(DH, DH).astype(BF16)
        carried = jnp.dot(qs_ref[:, cols], state, preferred_element_type=F32)
        att = intra_ref[:, cols] + carried * jnp.exp(cum_ref[:, lane : lane + 1])
        square = jnp.mean(att * att, axis=-1, keepdims=True)
        gain = gain_ref[pl.ds(core * HC + h, 1), :]
        out[:, cols] = (att * lax.rsqrt(square + 1e-06) * gain).astype(BF16)
    mine_ref[...] = out[span(core, BLK), :]
    yours_ref[...] = out[span(1 - core, BLK), :]
    fetch.wait()


def finish(place, layer, pieces, intra, cum, qs, gain, wo):
    if layer:
        intra, qs = in_hbm(intra), in_hbm(qs)
    args = (pieces, intra, cum, qs, gain)
    return call(
        lambda *refs: finish_kernel(layer, *refs), "finish", place, (*args, in_hbm(wo)),
        (struct((BLK, HW), BF16), struct((BLK, HW), BF16), pltpu.VMEM(WO_HALF, BF16)),
        in_specs=[whole(a.shape) for a in args] + [ANY],
        out_specs=[whole((BLK, HW)), whole((BLK, HW)), IN_VMEM],
        scratch=(pltpu.VMEM((TOK, HW), BF16), pltpu.SemaphoreType.DMA),
    )


def project_kernel(place, mine_ref, yours_ref, near_ref, w_ref, out_ref, rows, held, sem):
    core = place[0]
    step = pl.program_id(0)
    half = STEPS // 2
    fetch = pltpu.make_async_copy(w_ref.at[:, WO_HALF[1] :], held, sem)

    @pl.when(step == 0)
    def _():
        fetch.start()
        rows[:, span(core, HW)] = mine_ref[...]
        rows[:, span(1 - core, HW)] = yours_ref[...]

    @pl.when(step == half)
    def _():
        fetch.wait()

    def term(w):
        cols = span(step % half, KSTEP)
        part = jnp.dot(rows[...], w[:, cols], preferred_element_type=F32).astype(BF16)
        out_ref[0] = part[:, :WIDTH]
        out_ref[1] = part[:, WIDTH:]

    @pl.when(step < half)
    def _():
        term(near_ref)

    @pl.when(step >= half)
    def _():
        term(held)


def project(place, mine, yours, near, w):
    return call(
        project_kernel, "project", place, (mine, yours, near, in_hbm(w)),
        (struct((NHEAD, BLK, WIDTH), BF16),),
        grid=(STEPS,),
        in_specs=[whole(mine.shape), whole(yours.shape), IN_VMEM, ANY],
        out_specs=[pl.BlockSpec((2, BLK, WIDTH), lambda i, _: (i, 0, 0))],
        scratch=(
            pltpu.VMEM((BLK, 2 * HW), BF16), pltpu.VMEM(WO_HALF, BF16), pltpu.SemaphoreType.DMA,
        ),
    )[0]


def exchange(parts, axes):
    return lax.all_to_all(parts, axes, 0, 0)


def after(value, *others):
    return lax.optimization_barrier((value, *others))[0]


def rest(place, layer, before, intra, cum, qs, gain, w):
    gain = in_hbm(gain.reshape(2 * HC, DH))
    mine, yours, near = finish(place, layer, before, intra, cum, qs, gain, w)
    yours = lax.ppermute(yours, "c", SWAP)
    terms = exchange(project(place, mine, yours, near, w), ("x", "yl"))
    return jnp.sum(terms.astype(F32), axis=0)


def local(
    q1, k1, v1, decay1, gain_out1, wo1, stream_in, gain_in2, wq2, wk2, wv2, decay2, gain_out2, wo2
):
    core = lax.axis_index("c")
    place = jnp.stack([core, lax.axis_index("yh")]).astype(jnp.int32)

    def swapped(*arrays):
        return [lax.ppermute(a, "c", SWAP) for a in arrays]

    decays = jnp.concatenate([decay1.T, decay2.T], axis=0)
    other_k, other_v, other_decays = swapped(k1, v1, decays)
    pieces, ks, vs, cum, across = first_state(
        place, in_hbm(k1), other_k, in_hbm(v1), other_v, decays, other_decays
    )

    near, give = cut(place, wk2, wv2, wq2)
    far = lax.ppermute(near, "yh", SWAP)
    near_other, = swapped(give)
    q1 = after(q1, pieces)
    other_q, = swapped(q1)
    sums = after(exchange(pieces, ("yh", "z")), other_q, near_other)
    scanned = scan(place, sums)
    before = exchange(scanned, ("yh", "z"))
    far = after(far, scanned)
    far_other, = swapped(far[:, 3 * HW :])
    intra, qs = first_intra(place, q1, other_q, ks, vs, cum, across)
    before, intra, *parts = lax.optimization_barrier(
        (before, intra, near, near_other, far, far_other)
    )
    near, near_other, far, far_other = parts
    rows_kv, rows_q = pack(place, near, in_hbm(near_other), far, in_hbm(far_other))

    def gather(rows):
        return lax.all_gather(rows, "z", axis=1, tiled=True)

    wkv = gather(rows_kv)
    first_share = rest(place, 0, before, intra, cum, qs, gain_out1, wo1)
    stream = (stream_in.astype(F32) + first_share).astype(BF16)
    wq = gather(after(rows_q, stream))

    mine = exchange(jnp.broadcast_to(stream[None], (NHEAD, BLK, WIDTH)), ("x", "yl"))
    yours = lax.ppermute(mine, "c", SWAP)
    gain = gain_in2.reshape(NHEAD, 1, WIDTH)
    own, wkv = own_kv(place, mine, wkv, gain)
    pieces, ks, vs = second_state(place, yours, wkv, gain, own, cum)
    sums = exchange(pieces, ("yh", "z"))
    before = exchange(scan(place, sums), ("yh", "z"))
    intra, qs = second_intra(place, mine, yours, wq, gain, ks, vs, cum, across)
    second_share = rest(place, 1, before, intra, cum, qs, gain_out2, wo2)
    return (stream.astype(F32) + second_share).astype(BF16)


def solution(mesh):
    fine = Mesh(mesh.devices.reshape(2, 8, 2, 4, 2), ("yh", "z", "c", "x", "yl"))
    seq, head = ("yh", "z", "c"), ("x", "yl")
    both = P(seq, head)
    placed = (
        both, both, both, both, P(head), P(head, None), both, P(),
        both, both, both, both, P(head), P(head, None),
    )
    return jax.shard_map(local, mesh=fine, in_specs=placed, out_specs=both, check_vma=False)
```

```python
import jax
import jax.numpy as jnp
from jax import lax
from jax.experimental import pallas as pl
from jax.experimental.pallas import tpu as pltpu
from jax.sharding import Mesh
from jax.sharding import PartitionSpec as P

DH = 128
BLK = 256
TOK = 512
HC = 3
HW = HC * DH
NCHIP = 16
SUB = DH // NCHIP
PIECE = 32
WIDTH = 384
NHEAD = 8
STEPS = 4
KSTEP = 2 * WIDTH
SWAP = [(0, 1), (1, 0)]
VMEM = 16 * 1024 * 1024
F32 = jnp.float32
BF16 = jnp.bfloat16


def silu(u):
    return u / (1.0 + jnp.exp(-u))


def whole(shape):
    return pl.BlockSpec(shape, lambda *_: (0,) * len(shape))


def span(index, size):
    return pl.ds(pl.multiple_of(index * size, DH), size)


def call(kernel, name, place, args, outs, grid=(1,), in_specs=None, out_specs=None, scratch=(), flops=0):
    return pl.pallas_call(
        kernel,
        out_shape=outs,
        grid_spec=pltpu.PrefetchScalarGridSpec(
            num_scalar_prefetch=1,
            grid=grid,
            in_specs=in_specs or [whole(a.shape) for a in args],
            out_specs=out_specs or [whole(o.shape) for o in outs],
            scratch_shapes=scratch,
        ),
        compiler_params=pltpu.CompilerParams(vmem_limit_bytes=VMEM),
        cost_estimate=pl.CostEstimate(flops=flops, bytes_accessed=0, transcendentals=0),
        name=name,
    )(place, *args)


def struct(shape, dtype):
    return jax.ShapeDtypeStruct(shape, dtype)


def in_hbm(a):
    return pltpu.with_memory_space_constraint(a, pltpu.HBM)


def sum_decays(core, mine_ref, yours_ref, cum_ref, across_ref, rows):
    rows[...] = jnp.zeros_like(rows)
    rows[: 4 * HC, span(core, BLK)] = mine_ref[...]
    rows[: 4 * HC, span(1 - core, BLK)] = yours_ref[...]
    before = lax.broadcasted_iota(jnp.int32, (TOK, TOK), 0)
    after = lax.broadcasted_iota(jnp.int32, (TOK, TOK), 1)
    upper = (before <= after).astype(F32)
    sums = jnp.dot(rows[...], upper, preferred_element_type=F32, precision=lax.Precision.HIGHEST)
    first = jnp.where(core == 0, sums[0:HC], sums[HC : 2 * HC])
    second = jnp.where(core == 0, sums[2 * HC : 3 * HC], sums[3 * HC : 4 * HC])
    across = jnp.concatenate([first, second, jnp.zeros((2, TOK), F32)], axis=0)
    across_ref[...] = across
    cum_ref[...] = jnp.concatenate([across, jnp.zeros((DH - 8, TOK), F32)], axis=0).T


def make_pieces(ks, vs, cum_ref, layer, pieces_ref):
    states = []
    decays = jnp.zeros((SUB, DH), F32)
    slot = lax.broadcasted_iota(jnp.int32, (SUB, DH), 0)
    for h in range(HC):
        cols = slice(h * DH, (h + 1) * DH)
        lane = layer * HC + h
        ch = cum_ref[:, lane : lane + 1]
        last = ch[TOK - 1 : TOK]
        kt = (ks[:, cols].astype(F32) * jnp.exp(last - ch)).astype(BF16)
        state = lax.dot_general(kt, vs[:, cols], (((0,), (0,)), ((), ())), preferred_element_type=F32)
        states.append(state.reshape(NCHIP, SUB, DH))
        total = jnp.exp(last)
        high = total.astype(BF16).astype(F32)
        decays = jnp.where(slot == h, high, decays)
        decays = jnp.where(slot == HC + h, total - high, decays)
    states.append(jnp.broadcast_to(decays[None], (NCHIP, SUB, DH)))
    pieces_ref[...] = jnp.concatenate(states, axis=1).astype(BF16)


def make_intra(qs, ks, vs, cum_ref, across_ref, layer, intra_ref):
    lower = lax.broadcasted_iota(jnp.int32, (BLK, BLK), 0) >= lax.broadcasted_iota(
        jnp.int32, (BLK, BLK), 1
    )
    for h in range(HC):
        cols = slice(h * DH, (h + 1) * DH)
        lane = layer * HC + h
        for i in range(2):
            rows = slice(i * BLK, (i + 1) * BLK)
            total = None
            for j in range(i + 1):
                keys = slice(j * BLK, (j + 1) * BLK)
                scores = lax.dot_general(
                    qs[rows, cols], ks[keys, cols], (((1,), (1,)), ((), ())),
                    preferred_element_type=F32,
                )
                spread = cum_ref[rows, lane : lane + 1] - across_ref[lane : lane + 1, keys]
                if i == j:
                    factor = jnp.where(lower, jnp.exp(jnp.where(lower, spread, 0.0)), 0.0)
                else:
                    factor = jnp.exp(spread)
                weights = (scores * factor).astype(BF16)
                part = jnp.dot(weights, vs[keys, cols], preferred_element_type=F32)
                total = part if total is None else total + part
            intra_ref[rows, cols] = total


def both_cores(core, mine_ref, yours_ref, out):
    out[span(core, BLK), :] = silu(mine_ref[:, span(core, HW)].astype(F32)).astype(BF16)
    out[span(1 - core, BLK), :] = silu(yours_ref[:, span(core, HW)].astype(F32)).astype(BF16)


def first_state_kernel(
    place, k_ref, other_k_ref, v_ref, other_v_ref, decay_ref, other_decay_ref,
    pieces_ref, ks, vs, cum_ref, across_ref, rows,
):
    core = place[0]
    both_cores(core, k_ref, other_k_ref, ks)
    both_cores(core, v_ref, other_v_ref, vs)
    sum_decays(core, decay_ref, other_decay_ref, cum_ref, across_ref, rows)
    make_pieces(ks, vs, cum_ref, 0, pieces_ref)


IN_VMEM = pl.BlockSpec(memory_space=pltpu.VMEM)
ANY = pl.BlockSpec(memory_space=pl.ANY)
HEADS_OUT = pltpu.HBM((TOK, HW), BF16)
QUERY_OUT = struct((TOK, HW), BF16)
INTRA_OUT = struct((TOK, HW), F32)
WO_OUT = pltpu.VMEM((2 * HW, NHEAD * WIDTH), BF16)
WKV_OUT = pltpu.VMEM((2, NHEAD * WIDTH // 2, 2 * HW), BF16)
PIECES_OUT = struct((NCHIP, PIECE, DH), BF16)


def first_state(place, *args):
    outs = (PIECES_OUT, HEADS_OUT, HEADS_OUT, struct((TOK, DH), F32), struct((8, TOK), F32))
    scratch = (pltpu.VMEM((16, TOK), F32),)
    return call(first_state_kernel, "first_state", place, args, outs, scratch=scratch)


def first_intra_kernel(
    place, q_ref, other_ref, ks, vs, cum_ref, across_ref, intra_ref, qs
):
    core = place[0]
    both_cores(core, q_ref, other_ref, qs)
    make_intra(qs, ks, vs, cum_ref, across_ref, 0, intra_ref)


def first_intra(place, q, other, ks, vs, cum, across):
    args = (q, other, in_hbm(ks), in_hbm(vs), cum, across)
    return call(first_intra_kernel, "first_intra", place, args, (INTRA_OUT, QUERY_OUT))


def project_step(h_ref, w, gain_ref, acc, square, rows):
    step = pl.program_id(0)
    parts = []
    total = None
    for i in range(2):
        wide = h_ref[i].astype(F32)
        parts.append((wide * gain_ref[i]).astype(BF16))
        for n in range(WIDTH // DH):
            tile = wide[:, n * DH : (n + 1) * DH]
            total = tile * tile if total is None else total + tile * tile
    part = jnp.concatenate(parts, axis=1)

    term = jnp.dot(part, w, preferred_element_type=F32)

    @pl.when(step == 0)
    def _():
        square[rows, :] = total
        acc[rows, :] = term

    @pl.when(step > 0)
    def _():
        square[rows, :] += total
        acc[rows, :] += term


def row_scale(square):
    mean = jnp.sum(square, axis=-1, keepdims=True) / (NHEAD * WIDTH)
    return lax.rsqrt(mean + 1e-06)


def chunk_at(i, place):
    half = STEPS // 2
    return jnp.where(i < half, place[1] * half + i, (1 - place[1]) * half + i - half), 0, 0


def projection_specs(width):
    half = STEPS // 2
    return (
        pl.BlockSpec((2, BLK, WIDTH), chunk_at),
        pl.BlockSpec((1, KSTEP, width), lambda i, _: (i // half, i % half, 0)),
        pl.BlockSpec((2, 1, WIDTH), chunk_at),
    )


def weight_rows(w_ref):
    half = STEPS // 2
    step = pl.program_id(0)
    return w_ref.at[step // half, pl.ds(pl.multiple_of(step % half * KSTEP, KSTEP), KSTEP), :]


def own_kv_kernel(place, h_ref, w_ref, gain_ref, out_ref, held, acc, square, sems):
    step = pl.program_id(0)
    half = STEPS // 2

    def fetch(n):
        rows = pl.ds(n % half * KSTEP, KSTEP)
        return pltpu.make_async_copy(
            w_ref.at[n // half, rows, :], held.at[n // half, rows, :], sems.at[n]
        )

    @pl.when(step == 0)
    def _():
        for n in range(STEPS):
            fetch(n).start()

    for n in range(STEPS):

        @pl.when(step == n)
        def _(n=n):
            fetch(n).wait()

    project_step(h_ref, weight_rows(held)[...], gain_ref, acc, square, slice(0, BLK))

    @pl.when(step == STEPS - 1)
    def _():
        out_ref[...] = silu(acc[...] * row_scale(square[...])).astype(BF16)


def own_kv(place, h, w, gain):
    hs, _, gs = projection_specs(2 * HW)
    return call(
        own_kv_kernel, "own_kv", place, (h, in_hbm(w), gain),
        (struct((BLK, 2 * HW), BF16), WKV_OUT),
        grid=(STEPS,), in_specs=[hs, ANY, gs], out_specs=[whole((BLK, 2 * HW)), IN_VMEM],
        scratch=(
            pltpu.VMEM((BLK, 2 * HW), F32), pltpu.VMEM((BLK, DH), F32),
            pltpu.SemaphoreType.DMA((STEPS,)),
        ),
    )


def second_state_kernel(
    place, h_ref, w_ref, gain_ref, own_ref, cum_ref, pieces_ref, ks, vs, acc, square
):
    core = place[0]
    project_step(h_ref, weight_rows(w_ref)[...], gain_ref, acc, square, slice(0, BLK))

    @pl.when(pl.program_id(0) == STEPS - 1)
    def _():
        scale = row_scale(square[...])
        for n, dst in enumerate((ks, vs)):
            cols = slice(n * HW, (n + 1) * HW)
            dst[span(core, BLK), :] = own_ref[:, cols]
            dst[span(1 - core, BLK), :] = silu(acc[:, cols] * scale).astype(BF16)
        make_pieces(ks, vs, cum_ref, 1, pieces_ref)


def second_state(place, h, w, gain, own, cum):
    hs, _, gs = projection_specs(2 * HW)
    return call(
        second_state_kernel, "second_state", place, (h, w, gain, own, cum),
        (PIECES_OUT, HEADS_OUT, HEADS_OUT),
        grid=(STEPS,), in_specs=[hs, IN_VMEM, gs, whole(own.shape), whole(cum.shape)],
        scratch=(pltpu.VMEM((BLK, 2 * HW), F32), pltpu.VMEM((BLK, DH), F32)),
    )


def second_intra_kernel(
    place, mine_ref, yours_ref, w_ref, gain_ref, ks, vs, cum_ref, across_ref,
    intra_ref, qs, acc, square,
):
    core = place[0]
    for n, src in enumerate((mine_ref, yours_ref)):
        rows = slice(n * BLK, (n + 1) * BLK)
        project_step(src, w_ref[0], gain_ref, acc, square, rows)

    @pl.when(pl.program_id(0) == STEPS - 1)
    def _():
        act = silu(acc[...] * row_scale(square[...])).astype(BF16)
        qs[span(core, BLK), :] = act[:BLK]
        qs[span(1 - core, BLK), :] = act[BLK:]
        make_intra(qs, ks, vs, cum_ref, across_ref, 1, intra_ref)


def second_intra(place, mine, yours, w, gain, ks, vs, cum, across):
    hs, ws, gs = projection_specs(HW)
    return call(
        second_intra_kernel, "second_intra", place,
        (mine, yours, in_hbm(w), gain, in_hbm(ks), in_hbm(vs), cum, in_hbm(across)),
        (pltpu.HBM((TOK, HW), F32), HEADS_OUT),
        grid=(STEPS,),
        in_specs=[hs, hs, ws, gs] + [whole(a.shape) for a in (ks, vs, cum, across)],
        scratch=(pltpu.VMEM((TOK, HW), F32), pltpu.VMEM((TOK, DH), F32)),
    )


def cut_kernel(place, k_ref, v_ref, q_ref, both_ref, give_ref):
    core = place[0]
    for n, src in enumerate((k_ref, v_ref, q_ref)):
        both_ref[:, n * HW : (n + 1) * HW] = src[:, span(core, HW)]
        give = src[:, span(1 - core, HW)]
        both_ref[:, (n + 3) * HW : (n + 4) * HW] = give
        give_ref[:, n * HW : (n + 1) * HW] = give


def cut(place, *weights):
    rows = weights[0].shape[0]
    outs = (struct((rows, 6 * HW), BF16), struct((rows, 3 * HW), BF16))
    return call(cut_kernel, "cut", place, [in_hbm(w) for w in weights], outs)


def pack_kernel(place, near_ref, near_other_ref, far_ref, far_other_ref, kv_ref, wq_ref):
    core = place[0]
    rows = near_ref.shape[0]
    for n, pair in enumerate(((near_ref, near_other_ref), (far_ref, far_other_ref))):
        for src, owner in zip(pair, (core, 1 - core)):
            at = pl.ds(pl.multiple_of(owner * rows, rows), rows)
            kv_ref[n, at, :] = src[:, : 2 * HW]
            wq_ref[n, at, :] = src[:, 2 * HW : 3 * HW]


def pack(place, *parts):
    rows = 2 * parts[0].shape[0]
    outs = (pltpu.HBM((2, rows, 2 * HW), BF16), pltpu.HBM((2, rows, HW), BF16))
    return call(pack_kernel, "pack", place, parts, outs)


def scan_kernel(place, in_ref, out_ref):
    states = [jnp.zeros((SUB, DH), F32) for _ in range(HC)]
    empty = jnp.zeros((PIECE - HC * SUB, DH), F32)
    for p in range(NCHIP):
        piece = in_ref[p].astype(F32)
        out_ref[p] = jnp.concatenate(states + [empty], axis=0).astype(BF16)
        decays = piece[HC * SUB :]
        for h in range(HC):
            decay = decays[h : h + 1] + decays[HC + h : HC + h + 1]
            states[h] = states[h] * decay + piece[h * SUB : (h + 1) * SUB]


def scan(place, pieces):
    return call(scan_kernel, "scan", place, (pieces,), (PIECES_OUT,))[0]


def finish_kernel(
    layer, place, pieces_ref, intra_ref, cum_ref, qs_ref, gain_ref, wo_ref,
    mine_ref, yours_ref, held, out, sem,
):
    core = place[0]
    fetch = pltpu.make_async_copy(wo_ref, held, sem)
    fetch.start()
    pieces = pieces_ref[...].astype(F32)
    for h in range(HC):
        cols = slice(h * DH, (h + 1) * DH)
        lane = layer * HC + h
        state = pieces[:, h * SUB : (h + 1) * SUB].reshape(DH, DH).astype(BF16)
        carried = jnp.dot(qs_ref[:, cols], state, preferred_element_type=F32)
        att = intra_ref[:, cols] + carried * jnp.exp(cum_ref[:, lane : lane + 1])
        square = jnp.mean(att * att, axis=-1, keepdims=True)
        gain = gain_ref[pl.ds(core * HC + h, 1), :]
        out[:, cols] = (att * lax.rsqrt(square + 1e-06) * gain).astype(BF16)
    mine_ref[...] = out[span(core, BLK), :]
    yours_ref[...] = out[span(1 - core, BLK), :]
    fetch.wait()


def finish(place, layer, pieces, intra, cum, qs, gain, wo):
    if layer:
        intra, qs = in_hbm(intra), in_hbm(qs)
    args = (pieces, intra, cum, qs, gain)
    return call(
        lambda *refs: finish_kernel(layer, *refs), "finish", place, (*args, in_hbm(wo)),
        (struct((BLK, HW), BF16), struct((BLK, HW), BF16), WO_OUT),
        in_specs=[whole(a.shape) for a in args] + [ANY],
        out_specs=[whole((BLK, HW)), whole((BLK, HW)), IN_VMEM],
        scratch=(pltpu.VMEM((TOK, HW), BF16), pltpu.SemaphoreType.DMA),
    )


def project_kernel(place, mine_ref, yours_ref, w_ref, out_ref, rows):
    core = place[0]

    @pl.when(pl.program_id(0) == 0)
    def _():
        rows[:, span(core, HW)] = mine_ref[...]
        rows[:, span(1 - core, HW)] = yours_ref[...]

    cols = span(pl.program_id(0), KSTEP)
    term = jnp.dot(rows[...], w_ref[:, cols], preferred_element_type=F32).astype(BF16)
    out_ref[0] = term[:, :WIDTH]
    out_ref[1] = term[:, WIDTH:]


def project(place, mine, yours, w):
    return call(
        project_kernel, "project", place, (mine, yours, w),
        (struct((NHEAD, BLK, WIDTH), BF16),),
        grid=(STEPS,),
        in_specs=[
            whole(mine.shape), whole(yours.shape),
            IN_VMEM,
        ],
        out_specs=[pl.BlockSpec((2, BLK, WIDTH), lambda i, _: (i, 0, 0))],
        scratch=(pltpu.VMEM((BLK, 2 * HW), BF16),),
        flops=2 * BLK * 2 * HW * NHEAD * WIDTH,
    )[0]


def exchange(parts, axes):
    return lax.all_to_all(parts, axes, 0, 0)


def after(value, *others):
    return lax.optimization_barrier((value, *others))[0]


def rest(place, layer, before, intra, cum, qs, gain, w):
    mine, yours, w = finish(place, layer, before, intra, cum, qs, in_hbm(gain.reshape(2 * HC, DH)), w)
    yours = lax.ppermute(yours, "c", SWAP)
    terms = exchange(project(place, mine, yours, w), ("x", "yl"))
    return jnp.sum(terms.astype(F32), axis=0)


def local(
    q1, k1, v1, decay1, gain_out1, wo1, stream_in, gain_in2, wq2, wk2, wv2, decay2, gain_out2, wo2
):
    core = lax.axis_index("c")
    place = jnp.stack([core, lax.axis_index("yh")]).astype(jnp.int32)

    def swapped(*arrays):
        return [lax.ppermute(a, "c", SWAP) for a in arrays]

    decays = jnp.concatenate([decay1.T, decay2.T], axis=0)
    other_k, other_v, other_decays = swapped(k1, v1, decays)
    pieces, ks, vs, cum, across = first_state(
        place, in_hbm(k1), other_k, in_hbm(v1), other_v, decays, other_decays
    )

    near, give = cut(place, wk2, wv2, wq2)
    far = lax.ppermute(near, "yh", SWAP)
    far = after(far, pieces)
    near_other, far_other = swapped(give, far[:, 3 * HW :])
    rows_kv, rows_q = pack(place, near, near_other, far, far_other)
    q1 = after(q1, pieces)
    other_q, = swapped(q1)
    sums, _, rows_kv, rows_q = lax.optimization_barrier(
        (exchange(pieces, ("yh", "z")), other_q, rows_kv, rows_q)
    )
    before = exchange(scan(place, sums), ("yh", "z"))

    def gather(rows):
        return lax.all_gather(rows, "z", axis=1, tiled=True)

    wkv = gather(rows_kv)
    intra, qs = first_intra(place, q1, other_q, ks, vs, cum, across)
    first_share = rest(place, 0, before, intra, cum, qs, gain_out1, wo1)
    stream = (stream_in.astype(F32) + first_share).astype(BF16)
    wq = gather(after(rows_q, stream))

    mine = exchange(jnp.broadcast_to(stream[None], (NHEAD, BLK, WIDTH)), ("x", "yl"))
    yours = lax.ppermute(mine, "c", SWAP)
    gain = gain_in2.reshape(NHEAD, 1, WIDTH)
    own, wkv = own_kv(place, mine, wkv, gain)
    pieces, ks, vs = second_state(place, yours, wkv, gain, own, cum)
    sums = exchange(pieces, ("yh", "z"))
    before = exchange(scan(place, sums), ("yh", "z"))
    intra, qs = second_intra(place, mine, yours, wq, gain, ks, vs, cum, across)
    second_share = rest(place, 1, before, intra, cum, qs, gain_out2, wo2)
    return (stream.astype(F32) + second_share).astype(BF16)


def solution(mesh):
    fine = Mesh(mesh.devices.reshape(2, 8, 2, 4, 2), ("yh", "z", "c", "x", "yl"))
    seq, head = ("yh", "z", "c"), ("x", "yl")
    both = P(seq, head)
    placed = (
        both, both, both, both, P(head), P(head, None), both, P(),
        both, both, both, both, P(head), P(head, None),
    )
    return jax.shard_map(local, mesh=fine, in_specs=placed, out_specs=both, check_vma=False)
```

```python
import jax
import jax.numpy as jnp
from jax import lax
from jax.experimental import pallas as pl
from jax.experimental.pallas import tpu as pltpu
from jax.sharding import Mesh
from jax.sharding import PartitionSpec as P

DH = 128
BLK = 256
TOK = 512
HC = 3
HW = HC * DH
NCHIP = 16
SUB = DH // NCHIP
PIECE = 32
WIDTH = 384
NHEAD = 8
STEPS = 4
KSTEP = 2 * WIDTH
SWAP = [(0, 1), (1, 0)]
VMEM = 16 * 1024 * 1024
F32 = jnp.float32
BF16 = jnp.bfloat16


def silu(u):
    return u / (1.0 + jnp.exp(-u))


def whole(shape):
    return pl.BlockSpec(shape, lambda *_: (0,) * len(shape))


def span(index, size):
    return pl.ds(pl.multiple_of(index * size, DH), size)


def call(kernel, name, place, args, outs, grid=(1,), in_specs=None, out_specs=None, scratch=(), flops=0):
    return pl.pallas_call(
        kernel,
        out_shape=outs,
        grid_spec=pltpu.PrefetchScalarGridSpec(
            num_scalar_prefetch=1,
            grid=grid,
            in_specs=in_specs or [whole(a.shape) for a in args],
            out_specs=out_specs or [whole(o.shape) for o in outs],
            scratch_shapes=scratch,
        ),
        compiler_params=pltpu.CompilerParams(vmem_limit_bytes=VMEM),
        cost_estimate=pl.CostEstimate(flops=flops, bytes_accessed=0, transcendentals=0),
        name=name,
    )(place, *args)


def struct(shape, dtype):
    return jax.ShapeDtypeStruct(shape, dtype)


def in_hbm(a):
    return pltpu.with_memory_space_constraint(a, pltpu.HBM)


def sum_decays(core, mine_ref, yours_ref, cum_ref, across_ref, rows):
    rows[...] = jnp.zeros_like(rows)
    rows[: 4 * HC, span(core, BLK)] = mine_ref[...]
    rows[: 4 * HC, span(1 - core, BLK)] = yours_ref[...]
    before = lax.broadcasted_iota(jnp.int32, (TOK, TOK), 0)
    after = lax.broadcasted_iota(jnp.int32, (TOK, TOK), 1)
    upper = (before <= after).astype(BF16)
    left = rows[...]
    parts = []
    for _ in range(3):
        part = left.astype(BF16)
        parts.append(part)
        left = left - part.astype(F32)
    sums = jnp.dot(jnp.concatenate(parts, axis=0), upper, preferred_element_type=F32)
    sums = sums[:16] + (sums[16:32] + sums[32:])
    first = jnp.where(core == 0, sums[0:HC], sums[HC : 2 * HC])
    second = jnp.where(core == 0, sums[2 * HC : 3 * HC], sums[3 * HC : 4 * HC])
    across = jnp.concatenate([first, second, jnp.zeros((2, TOK), F32)], axis=0)
    across_ref[...] = across
    cum_ref[...] = jnp.concatenate([across, jnp.zeros((DH - 8, TOK), F32)], axis=0).T


def make_pieces(ks, vs, cum_ref, layer, pieces_ref):
    states = []
    decays = jnp.zeros((SUB, DH), F32)
    slot = lax.broadcasted_iota(jnp.int32, (SUB, DH), 0)
    for h in range(HC):
        cols = slice(h * DH, (h + 1) * DH)
        lane = layer * HC + h
        ch = cum_ref[:, lane : lane + 1]
        last = ch[TOK - 1 : TOK]
        kt = (ks[:, cols].astype(F32) * jnp.exp(last - ch)).astype(BF16)
        state = lax.dot_general(kt, vs[:, cols], (((0,), (0,)), ((), ())), preferred_element_type=F32)
        states.append(state.reshape(NCHIP, SUB, DH))
        total = jnp.exp(last)
        high = total.astype(BF16).astype(F32)
        decays = jnp.where(slot == h, high, decays)
        decays = jnp.where(slot == HC + h, total - high, decays)
    states.append(jnp.broadcast_to(decays[None], (NCHIP, SUB, DH)))
    pieces_ref[...] = jnp.concatenate(states, axis=1).astype(BF16)


def make_intra(qs, ks, vs, cum_ref, across_ref, layer, intra_ref):
    lower = lax.broadcasted_iota(jnp.int32, (BLK, BLK), 0) >= lax.broadcasted_iota(
        jnp.int32, (BLK, BLK), 1
    )
    for h in range(HC):
        cols = slice(h * DH, (h + 1) * DH)
        lane = layer * HC + h
        for i in range(2):
            rows = slice(i * BLK, (i + 1) * BLK)
            total = None
            for j in range(i + 1):
                keys = slice(j * BLK, (j + 1) * BLK)
                scores = lax.dot_general(
                    qs[rows, cols], ks[keys, cols], (((1,), (1,)), ((), ())),
                    preferred_element_type=F32,
                )
                spread = cum_ref[rows, lane : lane + 1] - across_ref[lane : lane + 1, keys]
                if i == j:
                    factor = jnp.where(lower, jnp.exp(jnp.where(lower, spread, 0.0)), 0.0)
                else:
                    factor = jnp.exp(spread)
                weights = (scores * factor).astype(BF16)
                part = jnp.dot(weights, vs[keys, cols], preferred_element_type=F32)
                total = part if total is None else total + part
            intra_ref[rows, cols] = total


def both_cores(core, mine_ref, yours_ref, out):
    out[span(core, BLK), :] = silu(mine_ref[:, span(core, HW)].astype(F32)).astype(BF16)
    out[span(1 - core, BLK), :] = silu(yours_ref[:, span(core, HW)].astype(F32)).astype(BF16)


def first_state_kernel(
    place, k_ref, other_k_ref, v_ref, other_v_ref, decay_ref, other_decay_ref,
    pieces_ref, ks, vs, cum_ref, across_ref, rows,
):
    core = place[0]
    both_cores(core, k_ref, other_k_ref, ks)
    both_cores(core, v_ref, other_v_ref, vs)
    sum_decays(core, decay_ref, other_decay_ref, cum_ref, across_ref, rows)
    make_pieces(ks, vs, cum_ref, 0, pieces_ref)


IN_VMEM = pl.BlockSpec(memory_space=pltpu.VMEM)
ANY = pl.BlockSpec(memory_space=pl.ANY)
HEADS_OUT = pltpu.HBM((TOK, HW), BF16)
QUERY_OUT = struct((TOK, HW), BF16)
INTRA_OUT = struct((TOK, HW), F32)
WO_OUT = pltpu.VMEM((2 * HW, NHEAD * WIDTH), BF16)
WKV_OUT = pltpu.VMEM((2, NHEAD * WIDTH // 2, 2 * HW), BF16)
PIECES_OUT = struct((NCHIP, PIECE, DH), BF16)


def first_state(place, *args):
    outs = (PIECES_OUT, HEADS_OUT, HEADS_OUT, struct((TOK, DH), F32), struct((8, TOK), F32))
    scratch = (pltpu.VMEM((16, TOK), F32),)
    return call(first_state_kernel, "first_state", place, args, outs, scratch=scratch)


def first_intra_kernel(
    place, q_ref, other_ref, ks, vs, cum_ref, across_ref, intra_ref, qs
):
    core = place[0]
    both_cores(core, q_ref, other_ref, qs)
    make_intra(qs, ks, vs, cum_ref, across_ref, 0, intra_ref)


def first_intra(place, q, other, ks, vs, cum, across):
    args = (q, other, in_hbm(ks), in_hbm(vs), cum, across)
    return call(first_intra_kernel, "first_intra", place, args, (INTRA_OUT, QUERY_OUT))


def gained(h_ref, gain_ref):
    parts = []
    total = None
    for i in range(2):
        wide = h_ref[i].astype(F32)
        parts.append((wide * gain_ref[i]).astype(BF16))
        for n in range(WIDTH // DH):
            tile = wide[:, n * DH : (n + 1) * DH]
            total = tile * tile if total is None else total + tile * tile
    return jnp.concatenate(parts, axis=1), total


def project_step(h_refs, w, gain_ref, acc, square):
    step = pl.program_id(0)
    parts, totals = zip(*(gained(h_ref, gain_ref) for h_ref in h_refs))
    part, total = jnp.concatenate(parts, axis=0), jnp.concatenate(totals, axis=0)

    term = jnp.dot(part, w, preferred_element_type=F32)

    @pl.when(step == 0)
    def _():
        square[...] = total
        acc[...] = term

    @pl.when(step > 0)
    def _():
        square[...] += total
        acc[...] += term


def row_scale(square):
    mean = jnp.sum(square, axis=-1, keepdims=True) / (NHEAD * WIDTH)
    return lax.rsqrt(mean + 1e-06)


def chunk_at(i, place):
    half = STEPS // 2
    return jnp.where(i < half, place[1] * half + i, (1 - place[1]) * half + i - half), 0, 0


def projection_specs(width):
    half = STEPS // 2
    return (
        pl.BlockSpec((2, BLK, WIDTH), chunk_at),
        pl.BlockSpec((1, KSTEP, width), lambda i, _: (i // half, i % half, 0)),
        pl.BlockSpec((2, 1, WIDTH), chunk_at),
    )


def weight_rows(w_ref):
    half = STEPS // 2
    step = pl.program_id(0)
    return w_ref.at[step // half, pl.ds(pl.multiple_of(step % half * KSTEP, KSTEP), KSTEP), :]


def own_kv_kernel(place, h_ref, w_ref, gain_ref, out_ref, held, acc, square, sems):
    step = pl.program_id(0)
    half = STEPS // 2

    def fetch(n):
        rows = pl.ds(n % half * KSTEP, KSTEP)
        return pltpu.make_async_copy(
            w_ref.at[n // half, rows, :], held.at[n // half, rows, :], sems.at[n]
        )

    @pl.when(step == 0)
    def _():
        for n in range(STEPS):
            fetch(n).start()

    for n in range(STEPS):

        @pl.when(step == n)
        def _(n=n):
            fetch(n).wait()

    project_step([h_ref], weight_rows(held)[...], gain_ref, acc, square)

    @pl.when(step == STEPS - 1)
    def _():
        out_ref[...] = silu(acc[...] * row_scale(square[...])).astype(BF16)


def own_kv(place, h, w, gain):
    hs, _, gs = projection_specs(2 * HW)
    return call(
        own_kv_kernel, "own_kv", place, (h, in_hbm(w), gain),
        (struct((BLK, 2 * HW), BF16), WKV_OUT),
        grid=(STEPS,), in_specs=[hs, ANY, gs], out_specs=[whole((BLK, 2 * HW)), IN_VMEM],
        scratch=(
            pltpu.VMEM((BLK, 2 * HW), F32), pltpu.VMEM((BLK, DH), F32),
            pltpu.SemaphoreType.DMA((STEPS,)),
        ),
    )


def second_state_kernel(
    place, h_ref, w_ref, gain_ref, own_ref, cum_ref, pieces_ref, ks, vs, acc, square
):
    core = place[0]
    project_step([h_ref], weight_rows(w_ref)[...], gain_ref, acc, square)

    @pl.when(pl.program_id(0) == STEPS - 1)
    def _():
        scale = row_scale(square[...])
        for n, dst in enumerate((ks, vs)):
            cols = slice(n * HW, (n + 1) * HW)
            dst[span(core, BLK), :] = own_ref[:, cols]
            dst[span(1 - core, BLK), :] = silu(acc[:, cols] * scale).astype(BF16)
        make_pieces(ks, vs, cum_ref, 1, pieces_ref)


def second_state(place, h, w, gain, own, cum):
    hs, _, gs = projection_specs(2 * HW)
    return call(
        second_state_kernel, "second_state", place, (h, w, gain, own, cum),
        (PIECES_OUT, HEADS_OUT, HEADS_OUT),
        grid=(STEPS,), in_specs=[hs, IN_VMEM, gs, whole(own.shape), whole(cum.shape)],
        scratch=(pltpu.VMEM((BLK, 2 * HW), F32), pltpu.VMEM((BLK, DH), F32)),
    )


def second_intra_kernel(
    place, mine_ref, yours_ref, w_ref, gain_ref, ks, vs, cum_ref, across_ref,
    intra_ref, qs, acc, square,
):
    core = place[0]
    project_step([mine_ref, yours_ref], w_ref[0], gain_ref, acc, square)

    @pl.when(pl.program_id(0) == STEPS - 1)
    def _():
        act = silu(acc[...] * row_scale(square[...])).astype(BF16)
        qs[span(core, BLK), :] = act[:BLK]
        qs[span(1 - core, BLK), :] = act[BLK:]
        make_intra(qs, ks, vs, cum_ref, across_ref, 1, intra_ref)


def second_intra(place, mine, yours, w, gain, ks, vs, cum, across):
    hs, ws, gs = projection_specs(HW)
    return call(
        second_intra_kernel, "second_intra", place,
        (mine, yours, in_hbm(w), gain, in_hbm(ks), in_hbm(vs), cum, in_hbm(across)),
        (pltpu.HBM((TOK, HW), F32), HEADS_OUT),
        grid=(STEPS,),
        in_specs=[hs, hs, ws, gs] + [whole(a.shape) for a in (ks, vs, cum, across)],
        scratch=(pltpu.VMEM((TOK, HW), F32), pltpu.VMEM((TOK, DH), F32)),
    )


def cut_kernel(place, k_ref, v_ref, q_ref, both_ref, give_ref):
    core = place[0]
    for n, src in enumerate((k_ref, v_ref, q_ref)):
        both_ref[:, n * HW : (n + 1) * HW] = src[:, span(core, HW)]
        give = src[:, span(1 - core, HW)]
        both_ref[:, (n + 3) * HW : (n + 4) * HW] = give
        give_ref[:, n * HW : (n + 1) * HW] = give


def cut(place, *weights):
    rows = weights[0].shape[0]
    outs = (struct((rows, 6 * HW), BF16), struct((rows, 3 * HW), BF16))
    return call(cut_kernel, "cut", place, [in_hbm(w) for w in weights], outs)


def pack_kernel(place, near_ref, near_other_ref, far_ref, far_other_ref, kv_ref, wq_ref):
    core = place[0]
    rows = near_ref.shape[0]
    for n, pair in enumerate(((near_ref, near_other_ref), (far_ref, far_other_ref))):
        for src, owner in zip(pair, (core, 1 - core)):
            at = pl.ds(pl.multiple_of(owner * rows, rows), rows)
            kv_ref[n, at, :] = src[:, : 2 * HW]
            wq_ref[n, at, :] = src[:, 2 * HW : 3 * HW]


def pack(place, *parts):
    rows = 2 * parts[0].shape[0]
    outs = (pltpu.HBM((2, rows, 2 * HW), BF16), pltpu.HBM((2, rows, HW), BF16))
    return call(pack_kernel, "pack", place, parts, outs)


def scan_kernel(place, in_ref, out_ref):
    states = [jnp.zeros((SUB, DH), F32) for _ in range(HC)]
    empty = jnp.zeros((PIECE - HC * SUB, DH), F32)
    for p in range(NCHIP):
        piece = in_ref[p].astype(F32)
        out_ref[p] = jnp.concatenate(states + [empty], axis=0).astype(BF16)
        decays = piece[HC * SUB :]
        for h in range(HC):
            decay = decays[h : h + 1] + decays[HC + h : HC + h + 1]
            states[h] = states[h] * decay + piece[h * SUB : (h + 1) * SUB]


def scan(place, pieces):
    return call(scan_kernel, "scan", place, (pieces,), (PIECES_OUT,))[0]


def finish_kernel(
    layer, place, pieces_ref, cum_ref, intra_hbm, qs_hbm, gain_hbm, wo_ref,
    mine_ref, yours_ref, held, out, intra_ref, qs_ref, gain_ref, sems,
):
    core = place[0]
    pairs = ((intra_hbm, intra_ref), (qs_hbm, qs_ref), (gain_hbm, gain_ref), (wo_ref, held))
    fetches = [pltpu.make_async_copy(a, b, sems.at[n]) for n, (a, b) in enumerate(pairs)]
    for fetch in fetches:
        fetch.start()
    pieces = pieces_ref[...].astype(F32)
    states = [
        pieces[:, h * SUB : (h + 1) * SUB].reshape(DH, DH).astype(BF16) for h in range(HC)
    ]
    scales = [jnp.exp(cum_ref[:, layer * HC + h : layer * HC + h + 1]) for h in range(HC)]
    for fetch in fetches[:3]:
        fetch.wait()
    for h in range(HC):
        cols = slice(h * DH, (h + 1) * DH)
        carried = jnp.dot(qs_ref[:, cols], states[h], preferred_element_type=F32)
        att = intra_ref[:, cols] + carried * scales[h]
        square = jnp.mean(att * att, axis=-1, keepdims=True)
        gain = gain_ref[pl.ds(core * HC + h, 1), :]
        out[:, cols] = (att * lax.rsqrt(square + 1e-06) * gain).astype(BF16)
    mine_ref[...] = out[span(core, BLK), :]
    yours_ref[...] = out[span(1 - core, BLK), :]
    fetches[3].wait()


def finish(place, layer, pieces, intra, cum, qs, gain, wo):
    if layer:
        intra, qs = in_hbm(intra), in_hbm(qs)
    return call(
        lambda *refs: finish_kernel(layer, *refs), "finish", place,
        (pieces, cum, intra, qs, gain, in_hbm(wo)),
        (struct((BLK, HW), BF16), struct((BLK, HW), BF16), WO_OUT),
        in_specs=[whole(pieces.shape), whole(cum.shape)] + [ANY] * 4,
        out_specs=[whole((BLK, HW)), whole((BLK, HW)), IN_VMEM],
        scratch=(
            pltpu.VMEM((TOK, HW), BF16), pltpu.VMEM((TOK, HW), F32), pltpu.VMEM((TOK, HW), BF16),
            pltpu.VMEM((2 * HC, DH), F32), pltpu.SemaphoreType.DMA((4,)),
        ),
    )


def project_kernel(place, mine_ref, yours_ref, w_ref, out_ref, rows):
    core = place[0]

    @pl.when(pl.program_id(0) == 0)
    def _():
        rows[:, span(core, HW)] = mine_ref[...]
        rows[:, span(1 - core, HW)] = yours_ref[...]

    cols = span(pl.program_id(0), KSTEP)
    term = jnp.dot(rows[...], w_ref[:, cols], preferred_element_type=F32).astype(BF16)
    out_ref[0] = term[:, :WIDTH]
    out_ref[1] = term[:, WIDTH:]


def project(place, mine, yours, w):
    return call(
        project_kernel, "project", place, (mine, yours, w),
        (struct((NHEAD, BLK, WIDTH), BF16),),
        grid=(STEPS,),
        in_specs=[
            whole(mine.shape), whole(yours.shape),
            IN_VMEM,
        ],
        out_specs=[pl.BlockSpec((2, BLK, WIDTH), lambda i, _: (i, 0, 0))],
        scratch=(pltpu.VMEM((BLK, 2 * HW), BF16),),
        flops=2 * BLK * 2 * HW * NHEAD * WIDTH,
    )[0]


def exchange(parts, axes):
    return lax.all_to_all(parts, axes, 0, 0)


def after(value, *others):
    return lax.optimization_barrier((value, *others))[0]


def rest(place, layer, before, intra, cum, qs, gain, w):
    mine, yours, w = finish(place, layer, before, intra, cum, qs, in_hbm(gain.reshape(2 * HC, DH)), w)
    yours = lax.ppermute(yours, "c", SWAP)
    terms = exchange(project(place, mine, yours, w), ("x", "yl"))
    return jnp.sum(terms.astype(F32), axis=0)


def local(
    q1, k1, v1, decay1, gain_out1, wo1, stream_in, gain_in2, wq2, wk2, wv2, decay2, gain_out2, wo2
):
    core = lax.axis_index("c")
    place = jnp.stack([core, lax.axis_index("yh")]).astype(jnp.int32)

    def swapped(*arrays):
        return [lax.ppermute(a, "c", SWAP) for a in arrays]

    decays = jnp.concatenate([decay1.T, decay2.T], axis=0)
    other_k, other_v, other_decays = swapped(k1, v1, decays)
    pieces, ks, vs, cum, across = first_state(
        place, in_hbm(k1), other_k, in_hbm(v1), other_v, decays, other_decays
    )

    near, give = cut(place, wk2, wv2, wq2)
    far = lax.ppermute(near, "yh", SWAP)
    far = after(far, pieces)
    near_other, far_other = swapped(give, far[:, 3 * HW :])
    rows_kv, rows_q = pack(place, near, near_other, far, far_other)
    q1 = after(q1, pieces)
    other_q, = swapped(q1)
    sums, _, rows_kv, rows_q = lax.optimization_barrier(
        (exchange(pieces, ("yh", "z")), other_q, rows_kv, rows_q)
    )
    before = exchange(scan(place, sums), ("yh", "z"))

    def gather(rows):
        return lax.all_gather(rows, "z", axis=1, tiled=True)

    wkv = gather(rows_kv)
    intra, qs = first_intra(place, q1, other_q, ks, vs, cum, across)
    first_share = rest(place, 0, before, intra, cum, qs, gain_out1, wo1)
    stream = (stream_in.astype(F32) + first_share).astype(BF16)
    wq = gather(after(rows_q, stream))

    mine = exchange(jnp.broadcast_to(stream[None], (NHEAD, BLK, WIDTH)), ("x", "yl"))
    yours = lax.ppermute(mine, "c", SWAP)
    gain = gain_in2.reshape(NHEAD, 1, WIDTH)
    own, wkv = own_kv(place, mine, wkv, gain)
    pieces, ks, vs = second_state(place, yours, wkv, gain, own, cum)
    sums = exchange(pieces, ("yh", "z"))
    before = exchange(scan(place, sums), ("yh", "z"))
    intra, qs = second_intra(place, mine, yours, wq, gain, ks, vs, cum, across)
    second_share = rest(place, 1, before, intra, cum, qs, gain_out2, wo2)
    return (stream.astype(F32) + second_share).astype(BF16)


def solution(mesh):
    fine = Mesh(mesh.devices.reshape(2, 8, 2, 4, 2), ("yh", "z", "c", "x", "yl"))
    seq, head = ("yh", "z", "c"), ("x", "yl")
    both = P(seq, head)
    placed = (
        both, both, both, both, P(head), P(head, None), both, P(),
        both, both, both, both, P(head), P(head, None),
    )
    return jax.shard_map(local, mesh=fine, in_specs=placed, out_specs=both, check_vma=False)
```

```python
import jax
import jax.numpy as jnp
from jax import lax
from jax.experimental import pallas as pl
from jax.experimental.pallas import tpu as pltpu
from jax.sharding import Mesh
from jax.sharding import PartitionSpec as P

DH = 128
BLK = 256
TOK = 512
HC = 3
HW = HC * DH
NCHIP = 16
SUB = DH // NCHIP
PIECE = 32
WIDTH = 384
NHEAD = 8
STEPS = 4
KSTEP = 2 * WIDTH
SWAP = [(0, 1), (1, 0)]
VMEM = 16 * 1024 * 1024
F32 = jnp.float32
BF16 = jnp.bfloat16


def silu(u):
    return u / (1.0 + jnp.exp(-u))


def whole(shape):
    return pl.BlockSpec(shape, lambda *_: (0,) * len(shape))


def span(index, size):
    return pl.ds(pl.multiple_of(index * size, DH), size)


def call(kernel, name, place, args, outs, grid=(1,), in_specs=None, out_specs=None, scratch=(), flops=0):
    return pl.pallas_call(
        kernel,
        out_shape=outs,
        grid_spec=pltpu.PrefetchScalarGridSpec(
            num_scalar_prefetch=1,
            grid=grid,
            in_specs=in_specs or [whole(a.shape) for a in args],
            out_specs=out_specs or [whole(o.shape) for o in outs],
            scratch_shapes=scratch,
        ),
        compiler_params=pltpu.CompilerParams(vmem_limit_bytes=VMEM),
        cost_estimate=pl.CostEstimate(flops=flops, bytes_accessed=0, transcendentals=0),
        name=name,
    )(place, *args)


def struct(shape, dtype):
    return jax.ShapeDtypeStruct(shape, dtype)


def in_hbm(a):
    return pltpu.with_memory_space_constraint(a, pltpu.HBM)


def sum_decays(core, mine_ref, yours_ref, cum_ref, across_ref, rows):
    rows[...] = jnp.zeros_like(rows)
    rows[: 4 * HC, span(core, BLK)] = mine_ref[...]
    rows[: 4 * HC, span(1 - core, BLK)] = yours_ref[...]
    before = lax.broadcasted_iota(jnp.int32, (TOK, TOK), 0)
    after = lax.broadcasted_iota(jnp.int32, (TOK, TOK), 1)
    upper = (before <= after).astype(BF16)
    left = rows[...]
    parts = []
    for _ in range(3):
        part = left.astype(BF16)
        parts.append(part)
        left = left - part.astype(F32)
    sums = jnp.dot(jnp.concatenate(parts, axis=0), upper, preferred_element_type=F32)
    sums = sums[:16] + (sums[16:32] + sums[32:])
    first = jnp.where(core == 0, sums[0:HC], sums[HC : 2 * HC])
    second = jnp.where(core == 0, sums[2 * HC : 3 * HC], sums[3 * HC : 4 * HC])
    across = jnp.concatenate([first, second, jnp.zeros((2, TOK), F32)], axis=0)
    across_ref[...] = across
    cum_ref[...] = jnp.concatenate([across, jnp.zeros((DH - 8, TOK), F32)], axis=0).T


def make_pieces(ks, vs, cum_ref, layer, pieces_ref):
    states = []
    decays = jnp.zeros((SUB, DH), F32)
    slot = lax.broadcasted_iota(jnp.int32, (SUB, DH), 0)
    for h in range(HC):
        cols = slice(h * DH, (h + 1) * DH)
        lane = layer * HC + h
        ch = cum_ref[:, lane : lane + 1]
        last = ch[TOK - 1 : TOK]
        kt = (ks[:, cols].astype(F32) * jnp.exp(last - ch)).astype(BF16)
        state = lax.dot_general(kt, vs[:, cols], (((0,), (0,)), ((), ())), preferred_element_type=F32)
        states.append(state.reshape(NCHIP, SUB, DH))
        total = jnp.exp(last)
        high = total.astype(BF16).astype(F32)
        decays = jnp.where(slot == h, high, decays)
        decays = jnp.where(slot == HC + h, total - high, decays)
    states.append(jnp.broadcast_to(decays[None], (NCHIP, SUB, DH)))
    pieces_ref[...] = jnp.concatenate(states, axis=1).astype(BF16)


def make_intra(qs, ks, vs, cum_ref, across_ref, layer, intra_ref):
    lower = lax.broadcasted_iota(jnp.int32, (BLK, BLK), 0) >= lax.broadcasted_iota(
        jnp.int32, (BLK, BLK), 1
    )
    for h in range(HC):
        cols = slice(h * DH, (h + 1) * DH)
        lane = layer * HC + h
        for i in range(2):
            rows = slice(i * BLK, (i + 1) * BLK)
            total = None
            for j in range(i + 1):
                keys = slice(j * BLK, (j + 1) * BLK)
                scores = lax.dot_general(
                    qs[rows, cols], ks[keys, cols], (((1,), (1,)), ((), ())),
                    preferred_element_type=F32,
                )
                spread = cum_ref[rows, lane : lane + 1] - across_ref[lane : lane + 1, keys]
                if i == j:
                    factor = jnp.where(lower, jnp.exp(jnp.where(lower, spread, 0.0)), 0.0)
                else:
                    factor = jnp.exp(spread)
                weights = (scores * factor).astype(BF16)
                part = jnp.dot(weights, vs[keys, cols], preferred_element_type=F32)
                total = part if total is None else total + part
            intra_ref[rows, cols] = total


def both_cores(core, mine_ref, yours_ref, out):
    out[span(core, BLK), :] = silu(mine_ref[:, span(core, HW)].astype(F32)).astype(BF16)
    out[span(1 - core, BLK), :] = silu(yours_ref[:, span(core, HW)].astype(F32)).astype(BF16)


def first_state_kernel(
    place, k_ref, other_k_ref, v_ref, other_v_ref, decay_ref, other_decay_ref,
    pieces_ref, ks, vs, cum_ref, across_ref, rows,
):
    core = place[0]
    both_cores(core, k_ref, other_k_ref, ks)
    both_cores(core, v_ref, other_v_ref, vs)
    sum_decays(core, decay_ref, other_decay_ref, cum_ref, across_ref, rows)
    make_pieces(ks, vs, cum_ref, 0, pieces_ref)


IN_VMEM = pl.BlockSpec(memory_space=pltpu.VMEM)
ANY = pl.BlockSpec(memory_space=pl.ANY)
HEADS_OUT = pltpu.HBM((TOK, HW), BF16)
QUERY_OUT = struct((TOK, HW), BF16)
INTRA_OUT = struct((TOK, HW), F32)
WO_OUT = pltpu.VMEM((2 * HW, NHEAD * WIDTH), BF16)
WKV_OUT = pltpu.VMEM((2, NHEAD * WIDTH // 2, 2 * HW), BF16)
PIECES_OUT = struct((NCHIP, PIECE, DH), BF16)


def first_state(place, *args):
    outs = (PIECES_OUT, HEADS_OUT, HEADS_OUT, struct((TOK, DH), F32), struct((8, TOK), F32))
    scratch = (pltpu.VMEM((16, TOK), F32),)
    return call(first_state_kernel, "first_state", place, args, outs, scratch=scratch)


def first_intra_kernel(
    place, q_ref, other_ref, ks, vs, cum_ref, across_ref, intra_ref, qs
):
    core = place[0]
    both_cores(core, q_ref, other_ref, qs)
    make_intra(qs, ks, vs, cum_ref, across_ref, 0, intra_ref)


def first_intra(place, q, other, ks, vs, cum, across):
    args = (q, other, in_hbm(ks), in_hbm(vs), cum, across)
    return call(first_intra_kernel, "first_intra", place, args, (INTRA_OUT, QUERY_OUT))


def gained(h_ref, gain_ref):
    parts = []
    total = None
    for i in range(2):
        wide = h_ref[i].astype(F32)
        parts.append((wide * gain_ref[i]).astype(BF16))
        for n in range(WIDTH // DH):
            tile = wide[:, n * DH : (n + 1) * DH]
            total = tile * tile if total is None else total + tile * tile
    return jnp.concatenate(parts, axis=1), total


def project_step(h_refs, w, gain_ref, acc, square):
    step = pl.program_id(0)
    parts, totals = zip(*(gained(h_ref, gain_ref) for h_ref in h_refs))
    part, total = jnp.concatenate(parts, axis=0), jnp.concatenate(totals, axis=0)

    term = jnp.dot(part, w, preferred_element_type=F32)

    @pl.when(step == 0)
    def _():
        square[...] = total
        acc[...] = term

    @pl.when(step > 0)
    def _():
        square[...] += total
        acc[...] += term


def row_scale(square):
    mean = jnp.sum(square, axis=-1, keepdims=True) / (NHEAD * WIDTH)
    return lax.rsqrt(mean + 1e-06)


def chunk_at(i, place):
    half = STEPS // 2
    return jnp.where(i < half, place[1] * half + i, (1 - place[1]) * half + i - half), 0, 0


def projection_specs(width):
    half = STEPS // 2
    return (
        pl.BlockSpec((2, BLK, WIDTH), chunk_at),
        pl.BlockSpec((1, KSTEP, width), lambda i, _: (i // half, i % half, 0)),
        pl.BlockSpec((2, 1, WIDTH), chunk_at),
    )


def weight_rows(w_ref):
    half = STEPS // 2
    step = pl.program_id(0)
    return w_ref.at[step // half, pl.ds(pl.multiple_of(step % half * KSTEP, KSTEP), KSTEP), :]


def own_kv_kernel(place, h_ref, w_ref, gain_ref, out_ref, held, acc, square, sems):
    step = pl.program_id(0)
    half = STEPS // 2

    def fetch(n):
        rows = pl.ds(n % half * KSTEP, KSTEP)
        return pltpu.make_async_copy(
            w_ref.at[n // half, rows, :], held.at[n // half, rows, :], sems.at[n]
        )

    @pl.when(step == 0)
    def _():
        for n in range(STEPS):
            fetch(n).start()

    for n in range(STEPS):

        @pl.when(step == n)
        def _(n=n):
            fetch(n).wait()

    project_step([h_ref], weight_rows(held)[...], gain_ref, acc, square)

    @pl.when(step == STEPS - 1)
    def _():
        out_ref[...] = silu(acc[...] * row_scale(square[...])).astype(BF16)


def own_kv(place, h, w, gain):
    hs, _, gs = projection_specs(2 * HW)
    return call(
        own_kv_kernel, "own_kv", place, (h, in_hbm(w), gain),
        (struct((BLK, 2 * HW), BF16), WKV_OUT),
        grid=(STEPS,), in_specs=[hs, ANY, gs], out_specs=[whole((BLK, 2 * HW)), IN_VMEM],
        scratch=(
            pltpu.VMEM((BLK, 2 * HW), F32), pltpu.VMEM((BLK, DH), F32),
            pltpu.SemaphoreType.DMA((STEPS,)),
        ),
    )


def second_state_kernel(
    place, h_ref, w_ref, gain_ref, own_ref, cum_ref, pieces_ref, ks, vs, acc, square
):
    core = place[0]
    project_step([h_ref], weight_rows(w_ref)[...], gain_ref, acc, square)

    @pl.when(pl.program_id(0) == STEPS - 1)
    def _():
        scale = row_scale(square[...])
        for n, dst in enumerate((ks, vs)):
            cols = slice(n * HW, (n + 1) * HW)
            dst[span(core, BLK), :] = own_ref[:, cols]
            dst[span(1 - core, BLK), :] = silu(acc[:, cols] * scale).astype(BF16)
        make_pieces(ks, vs, cum_ref, 1, pieces_ref)


def second_state(place, h, w, gain, own, cum):
    hs, _, gs = projection_specs(2 * HW)
    return call(
        second_state_kernel, "second_state", place, (h, w, gain, own, cum),
        (PIECES_OUT, HEADS_OUT, HEADS_OUT),
        grid=(STEPS,), in_specs=[hs, IN_VMEM, gs, whole(own.shape), whole(cum.shape)],
        scratch=(pltpu.VMEM((BLK, 2 * HW), F32), pltpu.VMEM((BLK, DH), F32)),
    )


def second_intra_kernel(
    place, mine_ref, yours_ref, w_ref, gain_ref, ks, vs, cum_ref, across_ref,
    intra_ref, qs, acc, square,
):
    core = place[0]
    project_step([mine_ref, yours_ref], w_ref[0], gain_ref, acc, square)

    @pl.when(pl.program_id(0) == STEPS - 1)
    def _():
        act = silu(acc[...] * row_scale(square[...])).astype(BF16)
        qs[span(core, BLK), :] = act[:BLK]
        qs[span(1 - core, BLK), :] = act[BLK:]
        make_intra(qs, ks, vs, cum_ref, across_ref, 1, intra_ref)


def second_intra(place, mine, yours, w, gain, ks, vs, cum, across):
    hs, ws, gs = projection_specs(HW)
    return call(
        second_intra_kernel, "second_intra", place,
        (mine, yours, in_hbm(w), gain, in_hbm(ks), in_hbm(vs), cum, in_hbm(across)),
        (pltpu.HBM((TOK, HW), F32), HEADS_OUT),
        grid=(STEPS,),
        in_specs=[hs, hs, ws, gs] + [whole(a.shape) for a in (ks, vs, cum, across)],
        scratch=(pltpu.VMEM((TOK, HW), F32), pltpu.VMEM((TOK, DH), F32)),
    )


def cut_kernel(place, k_ref, v_ref, q_ref, both_ref, give_ref):
    core = place[0]
    for n, src in enumerate((k_ref, v_ref, q_ref)):
        both_ref[:, n * HW : (n + 1) * HW] = src[:, span(core, HW)]
        give = src[:, span(1 - core, HW)]
        both_ref[:, (n + 3) * HW : (n + 4) * HW] = give
        give_ref[:, n * HW : (n + 1) * HW] = give


def cut(place, *weights):
    rows = weights[0].shape[0]
    outs = (struct((rows, 6 * HW), BF16), struct((rows, 3 * HW), BF16))
    return call(cut_kernel, "cut", place, [in_hbm(w) for w in weights], outs)


def pack_kernel(place, near_ref, near_other_ref, far_ref, far_other_ref, kv_ref, wq_ref):
    core = place[0]
    rows = near_ref.shape[0]
    for n, pair in enumerate(((near_ref, near_other_ref), (far_ref, far_other_ref))):
        for src, owner in zip(pair, (core, 1 - core)):
            at = pl.ds(pl.multiple_of(owner * rows, rows), rows)
            kv_ref[n, at, :] = src[:, : 2 * HW]
            wq_ref[n, at, :] = src[:, 2 * HW : 3 * HW]


def pack(place, *parts):
    rows = 2 * parts[0].shape[0]
    outs = (pltpu.HBM((2, rows, 2 * HW), BF16), pltpu.HBM((2, rows, HW), BF16))
    return call(pack_kernel, "pack", place, parts, outs)


def scan_kernel(place, in_ref, out_ref):
    states = [jnp.zeros((SUB, DH), F32) for _ in range(HC)]
    empty = jnp.zeros((PIECE - HC * SUB, DH), F32)
    for p in range(NCHIP):
        piece = in_ref[p].astype(F32)
        out_ref[p] = jnp.concatenate(states + [empty], axis=0).astype(BF16)
        decays = piece[HC * SUB :]
        for h in range(HC):
            decay = decays[h : h + 1] + decays[HC + h : HC + h + 1]
            states[h] = states[h] * decay + piece[h * SUB : (h + 1) * SUB]


def scan(place, pieces):
    return call(scan_kernel, "scan", place, (pieces,), (PIECES_OUT,))[0]


def finish_kernel(layer, own, place, pieces_ref, cum_ref, intra_hbm, qs_hbm, gain_hbm, *refs):
    core = place[0]
    rows = span(core if own else 1 - core, BLK)
    if own:
        wo_ref, out_ref, held, intra_ref, qs_ref, gain_ref, sems = refs
    else:
        out_ref, intra_ref, qs_ref, gain_ref, sems = refs
    pairs = [(intra_hbm.at[rows, :], intra_ref), (qs_hbm.at[rows, :], qs_ref), (gain_hbm, gain_ref)]
    if own:
        pairs.append((wo_ref, held))
    fetches = [pltpu.make_async_copy(a, b, sems.at[n]) for n, (a, b) in enumerate(pairs)]
    for fetch in fetches:
        fetch.start()
    pieces = pieces_ref[...].astype(F32)
    cum = cum_ref[rows, :]
    states = [
        pieces[:, h * SUB : (h + 1) * SUB].reshape(DH, DH).astype(BF16) for h in range(HC)
    ]
    scales = [jnp.exp(cum[:, layer * HC + h : layer * HC + h + 1]) for h in range(HC)]
    for fetch in fetches[:3]:
        fetch.wait()
    for h in range(HC):
        cols = slice(h * DH, (h + 1) * DH)
        carried = jnp.dot(qs_ref[:, cols], states[h], preferred_element_type=F32)
        att = intra_ref[:, cols] + carried * scales[h]
        square = jnp.mean(att * att, axis=-1, keepdims=True)
        gain = gain_ref[pl.ds(core * HC + h, 1), :]
        out_ref[:, cols] = (att * lax.rsqrt(square + 1e-06) * gain).astype(BF16)
    for fetch in fetches[3:]:
        fetch.wait()


def finish(place, layer, own, pieces, intra, cum, qs, gain, *wo):
    if layer:
        intra, qs = in_hbm(intra), in_hbm(qs)
    wo = [in_hbm(w) for w in wo]
    outs = (struct((BLK, HW), BF16),) + (WO_OUT,) * len(wo)
    return call(
        lambda *refs: finish_kernel(layer, own, *refs), "finish_own" if own else "finish_other",
        place, (pieces, cum, intra, qs, gain, *wo), outs,
        in_specs=[whole(pieces.shape), whole(cum.shape)] + [ANY] * (3 + len(wo)),
        out_specs=[whole((BLK, HW))] + [IN_VMEM] * len(wo),
        scratch=(
            pltpu.VMEM((BLK, HW), F32), pltpu.VMEM((BLK, HW), BF16),
            pltpu.VMEM((2 * HC, DH), F32), pltpu.SemaphoreType.DMA((4,)),
        ),
    )


def project_kernel(place, mine_ref, yours_ref, w_ref, out_ref, rows):
    core = place[0]

    @pl.when(pl.program_id(0) == 0)
    def _():
        rows[:, span(core, HW)] = mine_ref[...]
        rows[:, span(1 - core, HW)] = yours_ref[...]

    cols = span(pl.program_id(0), KSTEP)
    term = jnp.dot(rows[...], w_ref[:, cols], preferred_element_type=F32).astype(BF16)
    out_ref[0] = term[:, :WIDTH]
    out_ref[1] = term[:, WIDTH:]


def project(place, mine, yours, w):
    return call(
        project_kernel, "project", place, (mine, yours, w),
        (struct((NHEAD, BLK, WIDTH), BF16),),
        grid=(STEPS,),
        in_specs=[
            whole(mine.shape), whole(yours.shape),
            IN_VMEM,
        ],
        out_specs=[pl.BlockSpec((2, BLK, WIDTH), lambda i, _: (i, 0, 0))],
        scratch=(pltpu.VMEM((BLK, 2 * HW), BF16),),
        flops=2 * BLK * 2 * HW * NHEAD * WIDTH,
    )[0]


def exchange(parts, axes):
    return lax.all_to_all(parts, axes, 0, 0)


def after(value, *others):
    return lax.optimization_barrier((value, *others))[0]


def rest(place, layer, before, intra, cum, qs, gain, w):
    parts = (before, intra, cum, qs, in_hbm(gain.reshape(2 * HC, DH)))
    yours, = finish(place, layer, False, *parts)
    yours = lax.ppermute(yours, "c", SWAP)
    mine, w = finish(place, layer, True, *parts, w)
    terms = exchange(project(place, mine, yours, w), ("x", "yl"))
    return jnp.sum(terms.astype(F32), axis=0)


def local(
    q1, k1, v1, decay1, gain_out1, wo1, stream_in, gain_in2, wq2, wk2, wv2, decay2, gain_out2, wo2
):
    core = lax.axis_index("c")
    place = jnp.stack([core, lax.axis_index("yh")]).astype(jnp.int32)

    def swapped(*arrays):
        return [lax.ppermute(a, "c", SWAP) for a in arrays]

    decays = jnp.concatenate([decay1.T, decay2.T], axis=0)
    other_k, other_v, other_decays = swapped(k1, v1, decays)
    pieces, ks, vs, cum, across = first_state(
        place, in_hbm(k1), other_k, in_hbm(v1), other_v, decays, other_decays
    )

    near, give = cut(place, wk2, wv2, wq2)
    far = lax.ppermute(near, "yh", SWAP)
    far = after(far, pieces)
    near_other, far_other = swapped(give, far[:, 3 * HW :])
    rows_kv, rows_q = pack(place, near, near_other, far, far_other)
    q1 = after(q1, pieces)
    other_q, = swapped(q1)
    sums, _, rows_kv, rows_q = lax.optimization_barrier(
        (exchange(pieces, ("yh", "z")), other_q, rows_kv, rows_q)
    )
    before = exchange(scan(place, sums), ("yh", "z"))

    def gather(rows):
        return lax.all_gather(rows, "z", axis=1, tiled=True)

    wkv = gather(rows_kv)
    intra, qs = first_intra(place, q1, other_q, ks, vs, cum, across)
    first_share = rest(place, 0, before, intra, cum, qs, gain_out1, wo1)
    stream = (stream_in.astype(F32) + first_share).astype(BF16)
    wq = gather(after(rows_q, stream))

    mine = exchange(jnp.broadcast_to(stream[None], (NHEAD, BLK, WIDTH)), ("x", "yl"))
    yours = lax.ppermute(mine, "c", SWAP)
    gain = gain_in2.reshape(NHEAD, 1, WIDTH)
    own, wkv = own_kv(place, mine, wkv, gain)
    pieces, ks, vs = second_state(place, yours, wkv, gain, own, cum)
    sums = exchange(pieces, ("yh", "z"))
    before = exchange(scan(place, sums), ("yh", "z"))
    intra, qs = second_intra(place, mine, yours, wq, gain, ks, vs, cum, across)
    second_share = rest(place, 1, before, intra, cum, qs, gain_out2, wo2)
    return (stream.astype(F32) + second_share).astype(BF16)


def solution(mesh):
    fine = Mesh(mesh.devices.reshape(2, 8, 2, 4, 2), ("yh", "z", "c", "x", "yl"))
    seq, head = ("yh", "z", "c"), ("x", "yl")
    both = P(seq, head)
    placed = (
        both, both, both, both, P(head), P(head, None), both, P(),
        both, both, both, both, P(head), P(head, None),
    )
    return jax.shard_map(local, mesh=fine, in_specs=placed, out_specs=both, check_vma=False)
```

```python
import jax
import jax.numpy as jnp
from jax import lax
from jax.experimental import pallas as pl
from jax.experimental.pallas import tpu as pltpu
from jax.sharding import Mesh
from jax.sharding import PartitionSpec as P

DH = 128
BLK = 256
TOK = 512
HC = 3
HW = HC * DH
NCHIP = 16
SUB = DH // NCHIP
PIECE = 32
WIDTH = 384
NHEAD = 8
STEPS = 4
KSTEP = 2 * WIDTH
PAIR = 2
QUAD = NHEAD // PAIR
SWAP = [(0, 1), (1, 0)]
VMEM = 24 * 1024 * 1024
F32 = jnp.float32
BF16 = jnp.bfloat16


def silu(u):
    return u / (1.0 + jnp.exp(-u))


def whole(shape):
    return pl.BlockSpec(shape, lambda *_: (0,) * len(shape))


def span(index, size):
    return pl.ds(pl.multiple_of(index * size, DH), size)


def call(kernel, name, place, args, outs, grid=(1,), in_specs=None, out_specs=None, scratch=(), flops=0):
    return pl.pallas_call(
        kernel,
        out_shape=outs,
        grid_spec=pltpu.PrefetchScalarGridSpec(
            num_scalar_prefetch=1,
            grid=grid,
            in_specs=in_specs or [whole(a.shape) for a in args],
            out_specs=out_specs or [whole(o.shape) for o in outs],
            scratch_shapes=scratch,
        ),
        compiler_params=pltpu.CompilerParams(vmem_limit_bytes=VMEM),
        cost_estimate=pl.CostEstimate(flops=flops, bytes_accessed=0, transcendentals=0),
        name=name,
    )(place, *args)


def struct(shape, dtype):
    return jax.ShapeDtypeStruct(shape, dtype)


def in_hbm(a):
    return pltpu.with_memory_space_constraint(a, pltpu.HBM)


def sum_decays(core, mine_ref, yours_ref, cum_ref, across_ref, rows):
    rows[...] = jnp.zeros_like(rows)
    rows[: 4 * HC, span(core, BLK)] = mine_ref[...]
    rows[: 4 * HC, span(1 - core, BLK)] = yours_ref[...]
    before = lax.broadcasted_iota(jnp.int32, (TOK, TOK), 0)
    after = lax.broadcasted_iota(jnp.int32, (TOK, TOK), 1)
    upper = (before <= after).astype(BF16)
    left = rows[...]
    parts = []
    for _ in range(3):
        part = left.astype(BF16)
        parts.append(part)
        left = left - part.astype(F32)
    sums = jnp.dot(jnp.concatenate(parts, axis=0), upper, preferred_element_type=F32)
    sums = sums[:16] + (sums[16:32] + sums[32:])
    first = jnp.where(core == 0, sums[0:HC], sums[HC : 2 * HC])
    second = jnp.where(core == 0, sums[2 * HC : 3 * HC], sums[3 * HC : 4 * HC])
    across = jnp.concatenate([first, second, jnp.zeros((2, TOK), F32)], axis=0)
    across_ref[...] = across
    cum_ref[...] = jnp.concatenate([across, jnp.zeros((DH - 8, TOK), F32)], axis=0).T


def make_pieces(ks, vs, cum_ref, layer, pieces_ref):
    states = []
    decays = jnp.zeros((SUB, DH), F32)
    slot = lax.broadcasted_iota(jnp.int32, (SUB, DH), 0)
    for h in range(HC):
        cols = slice(h * DH, (h + 1) * DH)
        lane = layer * HC + h
        ch = cum_ref[:, lane : lane + 1]
        last = ch[TOK - 1 : TOK]
        kt = (ks[:, cols].astype(F32) * jnp.exp(last - ch)).astype(BF16)
        state = lax.dot_general(kt, vs[:, cols], (((0,), (0,)), ((), ())), preferred_element_type=F32)
        states.append(state.reshape(NCHIP, SUB, DH))
        total = jnp.exp(last)
        high = total.astype(BF16).astype(F32)
        decays = jnp.where(slot == h, high, decays)
        decays = jnp.where(slot == HC + h, total - high, decays)
    states.append(jnp.broadcast_to(decays[None], (NCHIP, SUB, DH)))
    pieces_ref[...] = jnp.concatenate(states, axis=1).astype(BF16)


def make_intra(qs, ks, vs, cum_ref, across_ref, layer, intra_ref):
    lower = lax.broadcasted_iota(jnp.int32, (BLK, BLK), 0) >= lax.broadcasted_iota(
        jnp.int32, (BLK, BLK), 1
    )
    for h in range(HC):
        cols = slice(h * DH, (h + 1) * DH)
        lane = layer * HC + h
        for i in range(2):
            rows = slice(i * BLK, (i + 1) * BLK)
            total = None
            for j in range(i + 1):
                keys = slice(j * BLK, (j + 1) * BLK)
                scores = lax.dot_general(
                    qs[rows, cols], ks[keys, cols], (((1,), (1,)), ((), ())),
                    preferred_element_type=F32,
                )
                spread = cum_ref[rows, lane : lane + 1] - across_ref[lane : lane + 1, keys]
                if i == j:
                    factor = jnp.where(lower, jnp.exp(jnp.where(lower, spread, 0.0)), 0.0)
                else:
                    factor = jnp.exp(spread)
                weights = (scores * factor).astype(BF16)
                part = jnp.dot(weights, vs[keys, cols], preferred_element_type=F32)
                total = part if total is None else total + part
            intra_ref[rows, cols] = total


def both_cores(core, mine_ref, yours_ref, out):
    out[span(core, BLK), :] = silu(mine_ref[...].astype(F32)).astype(BF16)
    out[span(1 - core, BLK), :] = silu(yours_ref[...].astype(F32)).astype(BF16)


HALF = pl.BlockSpec((BLK, HW), lambda _, place: (0, place[0]))


def first_state_kernel(
    place, k_ref, other_k_ref, v_ref, other_v_ref, decay_ref, other_decay_ref,
    pieces_ref, ks, vs, cum_ref, across_ref, rows,
):
    core = place[0]
    both_cores(core, k_ref, other_k_ref, ks)
    both_cores(core, v_ref, other_v_ref, vs)
    sum_decays(core, decay_ref, other_decay_ref, cum_ref, across_ref, rows)
    make_pieces(ks, vs, cum_ref, 0, pieces_ref)


IN_VMEM = pl.BlockSpec(memory_space=pltpu.VMEM)
ANY = pl.BlockSpec(memory_space=pl.ANY)
HEADS_OUT = pltpu.HBM((TOK, HW), BF16)
QUERY_OUT = struct((TOK, HW), BF16)
INTRA_OUT = struct((TOK, HW), F32)
WO_OUT = pltpu.VMEM((2 * HW, NHEAD * WIDTH), BF16)
WKV_OUT = pltpu.VMEM((2, NHEAD * WIDTH // 2, 2 * HW), BF16)
PIECES_OUT = struct((NCHIP, PIECE, DH), BF16)


def first_state(place, *args):
    outs = (PIECES_OUT, HEADS_OUT, HEADS_OUT, struct((TOK, DH), F32), struct((8, TOK), F32))
    scratch = (pltpu.VMEM((16, TOK), F32),)
    specs = [HALF] * 4 + [whole(a.shape) for a in args[4:]]
    return call(
        first_state_kernel, "first_state", place, args, outs, in_specs=specs, scratch=scratch
    )


def first_intra_kernel(
    place, q_ref, other_ref, ks, vs, cum_ref, across_ref, intra_ref, qs
):
    core = place[0]
    both_cores(core, q_ref, other_ref, qs)
    make_intra(qs, ks, vs, cum_ref, across_ref, 0, intra_ref)


def first_intra(place, q, other, ks, vs, cum, across):
    args = (q, other, in_hbm(ks), in_hbm(vs), cum, across)
    specs = [HALF] * 2 + [whole(a.shape) for a in args[2:]]
    outs = (INTRA_OUT, QUERY_OUT)
    return call(first_intra_kernel, "first_intra", place, args, outs, in_specs=specs)


def gained(h_ref, gain_ref):
    parts = []
    total = None
    for i in range(QUAD):
        wide = h_ref[i].astype(F32)
        parts.append((wide * gain_ref[i]).astype(BF16))
        for n in range(WIDTH // DH):
            tile = wide[:, n * DH : (n + 1) * DH]
            total = tile * tile if total is None else total + tile * tile
    return jnp.concatenate(parts, axis=1), total


def project_step(h_refs, w, gain_ref, acc, square):
    step = pl.program_id(0)
    parts, totals = zip(*(gained(h_ref, gain_ref) for h_ref in h_refs))
    part, total = jnp.concatenate(parts, axis=0), jnp.concatenate(totals, axis=0)

    term = jnp.dot(part, w, preferred_element_type=F32)

    @pl.when(step == 0)
    def _():
        square[...] = total
        acc[...] = term

    @pl.when(step > 0)
    def _():
        square[...] += total
        acc[...] += term


def row_scale(square):
    mean = jnp.sum(square, axis=-1, keepdims=True) / (NHEAD * WIDTH)
    return lax.rsqrt(mean + 1e-06)


def chunk_at(i, place):
    return jnp.where(i == 0, place[1], 1 - place[1]), 0, 0


def projection_specs(width):
    return (
        pl.BlockSpec((QUAD, BLK, WIDTH), chunk_at),
        pl.BlockSpec((1, QUAD * WIDTH, width), lambda i, _: (i, 0, 0)),
        pl.BlockSpec((QUAD, 1, WIDTH), chunk_at),
    )


def own_kv_kernel(place, h_ref, w_ref, gain_ref, out_ref, held, acc, square, sems):
    step = pl.program_id(0)
    fetches = [
        pltpu.make_async_copy(w_ref.at[n], held.at[n], sems.at[n]) for n in range(PAIR)
    ]

    @pl.when(step == 0)
    def _():
        for fetch in fetches:
            fetch.start()
        fetches[0].wait()

    @pl.when(step == 1)
    def _():
        fetches[1].wait()

    project_step([h_ref], held[step], gain_ref, acc, square)

    @pl.when(step == PAIR - 1)
    def _():
        out_ref[...] = silu(acc[...] * row_scale(square[...])).astype(BF16)


def own_kv(place, h, w, gain):
    hs, _, gs = projection_specs(2 * HW)
    return call(
        own_kv_kernel, "own_kv", place, (h, in_hbm(w), gain),
        (struct((BLK, 2 * HW), BF16), WKV_OUT),
        grid=(PAIR,), in_specs=[hs, ANY, gs], out_specs=[whole((BLK, 2 * HW)), IN_VMEM],
        scratch=(
            pltpu.VMEM((BLK, 2 * HW), F32), pltpu.VMEM((BLK, DH), F32),
            pltpu.SemaphoreType.DMA((PAIR,)),
        ),
    )


def second_state_kernel(
    place, h_ref, w_ref, gain_ref, own_ref, cum_ref, pieces_ref, ks, vs, acc, square
):
    core = place[0]
    project_step([h_ref], w_ref[pl.program_id(0)], gain_ref, acc, square)

    @pl.when(pl.program_id(0) == PAIR - 1)
    def _():
        scale = row_scale(square[...])
        for n, dst in enumerate((ks, vs)):
            cols = slice(n * HW, (n + 1) * HW)
            dst[span(core, BLK), :] = own_ref[:, cols]
            dst[span(1 - core, BLK), :] = silu(acc[:, cols] * scale).astype(BF16)
        make_pieces(ks, vs, cum_ref, 1, pieces_ref)


def second_state(place, h, w, gain, own, cum):
    hs, _, gs = projection_specs(2 * HW)
    return call(
        second_state_kernel, "second_state", place, (h, w, gain, own, cum),
        (PIECES_OUT, HEADS_OUT, HEADS_OUT),
        grid=(PAIR,), in_specs=[hs, IN_VMEM, gs, whole(own.shape), whole(cum.shape)],
        scratch=(pltpu.VMEM((BLK, 2 * HW), F32), pltpu.VMEM((BLK, DH), F32)),
    )


def second_intra_kernel(
    place, mine_ref, yours_ref, w_ref, gain_ref, ks, vs, cum_ref, across_ref,
    intra_ref, qs, acc, square,
):
    core = place[0]
    project_step([mine_ref, yours_ref], w_ref[0], gain_ref, acc, square)

    @pl.when(pl.program_id(0) == PAIR - 1)
    def _():
        act = silu(acc[...] * row_scale(square[...])).astype(BF16)
        qs[span(core, BLK), :] = act[:BLK]
        qs[span(1 - core, BLK), :] = act[BLK:]
        make_intra(qs, ks, vs, cum_ref, across_ref, 1, intra_ref)


def second_intra(place, mine, yours, w, gain, ks, vs, cum, across):
    hs, ws, gs = projection_specs(HW)
    return call(
        second_intra_kernel, "second_intra", place,
        (mine, yours, in_hbm(w), gain, in_hbm(ks), in_hbm(vs), cum, in_hbm(across)),
        (pltpu.HBM((TOK, HW), F32), HEADS_OUT),
        grid=(PAIR,),
        in_specs=[hs, hs, ws, gs] + [whole(a.shape) for a in (ks, vs, cum, across)],
        scratch=(pltpu.VMEM((TOK, HW), F32), pltpu.VMEM((TOK, DH), F32)),
    )


def cut_kernel(place, k_ref, v_ref, q_ref, both_ref, give_ref):
    core = place[0]
    for n, src in enumerate((k_ref, v_ref, q_ref)):
        both_ref[:, n * HW : (n + 1) * HW] = src[:, span(core, HW)]
        give = src[:, span(1 - core, HW)]
        both_ref[:, (n + 3) * HW : (n + 4) * HW] = give
        give_ref[:, n * HW : (n + 1) * HW] = give


def cut(place, *weights):
    rows = weights[0].shape[0]
    outs = (struct((rows, 6 * HW), BF16), struct((rows, 3 * HW), BF16))
    return call(cut_kernel, "cut", place, [in_hbm(w) for w in weights], outs)


def pack_kernel(place, near_ref, near_other_ref, far_ref, far_other_ref, kv_ref, wq_ref):
    core = place[0]
    rows = near_ref.shape[0]
    for n, pair in enumerate(((near_ref, near_other_ref), (far_ref, far_other_ref))):
        for src, owner in zip(pair, (core, 1 - core)):
            at = pl.ds(pl.multiple_of(owner * rows, rows), rows)
            kv_ref[n, at, :] = src[:, : 2 * HW]
            wq_ref[n, at, :] = src[:, 2 * HW : 3 * HW]


def pack(place, *parts):
    rows = 2 * parts[0].shape[0]
    outs = (pltpu.HBM((2, rows, 2 * HW), BF16), pltpu.HBM((2, rows, HW), BF16))
    return call(pack_kernel, "pack", place, parts, outs)


def scan_kernel(place, in_ref, out_ref):
    states = [jnp.zeros((SUB, DH), F32) for _ in range(HC)]
    empty = jnp.zeros((PIECE - HC * SUB, DH), F32)
    for p in range(NCHIP):
        piece = in_ref[p].astype(F32)
        out_ref[p] = jnp.concatenate(states + [empty], axis=0).astype(BF16)
        decays = piece[HC * SUB :]
        for h in range(HC):
            decay = decays[h : h + 1] + decays[HC + h : HC + h + 1]
            states[h] = states[h] * decay + piece[h * SUB : (h + 1) * SUB]


def scan(place, pieces):
    return call(scan_kernel, "scan", place, (pieces,), (PIECES_OUT,))[0]


def finish_kernel(
    layer, place, pieces_ref, cum_ref, intra_hbm, qs_hbm, gain_hbm, wo_ref,
    mine_ref, yours_ref, held, out, intra_ref, qs_ref, gain_ref, sems,
):
    core = place[0]
    pairs = ((intra_hbm, intra_ref), (qs_hbm, qs_ref), (gain_hbm, gain_ref), (wo_ref, held))
    fetches = [pltpu.make_async_copy(a, b, sems.at[n]) for n, (a, b) in enumerate(pairs)]
    for fetch in fetches:
        fetch.start()
    pieces = pieces_ref[...].astype(F32)
    states = [
        pieces[:, h * SUB : (h + 1) * SUB].reshape(DH, DH).astype(BF16) for h in range(HC)
    ]
    scales = [jnp.exp(cum_ref[:, layer * HC + h : layer * HC + h + 1]) for h in range(HC)]
    for fetch in fetches[:3]:
        fetch.wait()
    for h in range(HC):
        cols = slice(h * DH, (h + 1) * DH)
        carried = jnp.dot(qs_ref[:, cols], states[h], preferred_element_type=F32)
        att = intra_ref[:, cols] + carried * scales[h]
        square = jnp.mean(att * att, axis=-1, keepdims=True)
        gain = gain_ref[pl.ds(core * HC + h, 1), :]
        out[:, cols] = (att * lax.rsqrt(square + 1e-06) * gain).astype(BF16)
    mine_ref[...] = out[span(core, BLK), :]
    yours_ref[...] = out[span(1 - core, BLK), :]
    fetches[3].wait()


def finish(place, layer, pieces, intra, cum, qs, gain, wo):
    if layer:
        intra, qs = in_hbm(intra), in_hbm(qs)
    return call(
        lambda *refs: finish_kernel(layer, *refs), "finish", place,
        (pieces, cum, intra, qs, gain, in_hbm(wo)),
        (struct((BLK, HW), BF16), struct((BLK, HW), BF16), WO_OUT),
        in_specs=[whole(pieces.shape), whole(cum.shape)] + [ANY] * 4,
        out_specs=[whole((BLK, HW)), whole((BLK, HW)), IN_VMEM],
        scratch=(
            pltpu.VMEM((TOK, HW), BF16), pltpu.VMEM((TOK, HW), F32), pltpu.VMEM((TOK, HW), BF16),
            pltpu.VMEM((2 * HC, DH), F32), pltpu.SemaphoreType.DMA((4,)),
        ),
    )


def project_kernel(place, mine_ref, yours_ref, w_ref, out_ref, rows):
    core = place[0]

    @pl.when(pl.program_id(0) == 0)
    def _():
        rows[:, span(core, HW)] = mine_ref[...]
        rows[:, span(1 - core, HW)] = yours_ref[...]

    cols = span(pl.program_id(0), KSTEP)
    term = jnp.dot(rows[...], w_ref[:, cols], preferred_element_type=F32).astype(BF16)
    out_ref[0] = term[:, :WIDTH]
    out_ref[1] = term[:, WIDTH:]


def project(place, mine, yours, w):
    return call(
        project_kernel, "project", place, (mine, yours, w),
        (struct((NHEAD, BLK, WIDTH), BF16),),
        grid=(STEPS,),
        in_specs=[
            whole(mine.shape), whole(yours.shape),
            IN_VMEM,
        ],
        out_specs=[pl.BlockSpec((2, BLK, WIDTH), lambda i, _: (i, 0, 0))],
        scratch=(pltpu.VMEM((BLK, 2 * HW), BF16),),
        flops=2 * BLK * 2 * HW * NHEAD * WIDTH,
    )[0]


def exchange(parts, axes):
    return lax.all_to_all(parts, axes, 0, 0)


def after(value, *others):
    return lax.optimization_barrier((value, *others))[0]


def rest(place, layer, before, intra, cum, qs, gain, w):
    mine, yours, w = finish(place, layer, before, intra, cum, qs, in_hbm(gain.reshape(2 * HC, DH)), w)
    yours = lax.ppermute(yours, "c", SWAP)
    terms = exchange(project(place, mine, yours, w), ("x", "yl"))
    return jnp.sum(terms.astype(F32), axis=0)


def local(
    q1, k1, v1, decay1, gain_out1, wo1, stream_in, gain_in2, wq2, wk2, wv2, decay2, gain_out2, wo2
):
    core = lax.axis_index("c")
    place = jnp.stack([core, lax.axis_index("yh")]).astype(jnp.int32)

    def swapped(*arrays):
        return [lax.ppermute(a, "c", SWAP) for a in arrays]

    decays = jnp.concatenate([decay1.T, decay2.T], axis=0)
    other_k, other_v, other_decays = swapped(k1, v1, decays)
    pieces, ks, vs, cum, across = first_state(
        place, in_hbm(k1), other_k, in_hbm(v1), other_v, decays, other_decays
    )

    near, give = cut(place, wk2, wv2, wq2)
    far = lax.ppermute(near, "yh", SWAP)
    far = after(far, pieces)
    near_other, far_other = swapped(give, far[:, 3 * HW :])
    rows_kv, rows_q = pack(place, near, near_other, far, far_other)
    q1 = after(q1, pieces)
    other_q, = swapped(q1)
    sums, _, rows_kv, rows_q = lax.optimization_barrier(
        (exchange(pieces, ("yh", "z")), other_q, rows_kv, rows_q)
    )
    before = exchange(scan(place, sums), ("yh", "z"))

    def gather(rows):
        return lax.all_gather(rows, "z", axis=1, tiled=True)

    wkv = gather(rows_kv)
    intra, qs = first_intra(place, q1, other_q, ks, vs, cum, across)
    first_share = rest(place, 0, before, intra, cum, qs, gain_out1, wo1)
    stream = (stream_in.astype(F32) + first_share).astype(BF16)
    wq = gather(after(rows_q, stream))

    mine = exchange(jnp.broadcast_to(stream[None], (NHEAD, BLK, WIDTH)), ("x", "yl"))
    yours = lax.ppermute(mine, "c", SWAP)
    gain = gain_in2.reshape(NHEAD, 1, WIDTH)
    own, wkv = own_kv(place, mine, wkv, gain)
    pieces, ks, vs = second_state(place, yours, wkv, gain, own, cum)
    sums = exchange(pieces, ("yh", "z"))
    before = exchange(scan(place, sums), ("yh", "z"))
    intra, qs = second_intra(place, mine, yours, wq, gain, ks, vs, cum, across)
    second_share = rest(place, 1, before, intra, cum, qs, gain_out2, wo2)
    return (stream.astype(F32) + second_share).astype(BF16)


def solution(mesh):
    fine = Mesh(mesh.devices.reshape(2, 8, 2, 4, 2), ("yh", "z", "c", "x", "yl"))
    seq, head = ("yh", "z", "c"), ("x", "yl")
    both = P(seq, head)
    placed = (
        both, both, both, both, P(head), P(head, None), both, P(),
        both, both, both, both, P(head), P(head, None),
    )
    return jax.shard_map(local, mesh=fine, in_specs=placed, out_specs=both, check_vma=False)
```

```python
import jax
import jax.numpy as jnp
from jax import lax
from jax.experimental import pallas as pl
from jax.experimental.pallas import tpu as pltpu
from jax.sharding import Mesh
from jax.sharding import PartitionSpec as P

DH = 128
BLK = 256
TOK = 512
HC = 3
HW = HC * DH
NCHIP = 16
SUB = DH // NCHIP
PIECE = 32
WIDTH = 384
NHEAD = 8
STEPS = 2
KSTEP = NHEAD // STEPS * WIDTH
PAIR = 2
QUAD = NHEAD // PAIR
SWAP = [(0, 1), (1, 0)]
VMEM = 24 * 1024 * 1024
F32 = jnp.float32
BF16 = jnp.bfloat16


def silu(u):
    return u / (1.0 + jnp.exp(-u))


def whole(shape):
    return pl.BlockSpec(shape, lambda *_: (0,) * len(shape))


def span(index, size):
    return pl.ds(pl.multiple_of(index * size, DH), size)


def call(kernel, name, place, args, outs, grid=(1,), in_specs=None, out_specs=None, scratch=(), flops=0):
    return pl.pallas_call(
        kernel,
        out_shape=outs,
        grid_spec=pltpu.PrefetchScalarGridSpec(
            num_scalar_prefetch=1,
            grid=grid,
            in_specs=in_specs or [whole(a.shape) for a in args],
            out_specs=out_specs or [whole(o.shape) for o in outs],
            scratch_shapes=scratch,
        ),
        compiler_params=pltpu.CompilerParams(vmem_limit_bytes=VMEM),
        cost_estimate=pl.CostEstimate(flops=flops, bytes_accessed=0, transcendentals=0),
        name=name,
    )(place, *args)


def struct(shape, dtype):
    return jax.ShapeDtypeStruct(shape, dtype)


def in_hbm(a):
    return pltpu.with_memory_space_constraint(a, pltpu.HBM)


def sum_decays(core, mine_ref, yours_ref, cum_ref, across_ref, rows):
    rows[...] = jnp.zeros_like(rows)
    rows[: 4 * HC, span(core, BLK)] = mine_ref[...]
    rows[: 4 * HC, span(1 - core, BLK)] = yours_ref[...]
    before = lax.broadcasted_iota(jnp.int32, (TOK, TOK), 0)
    after = lax.broadcasted_iota(jnp.int32, (TOK, TOK), 1)
    upper = (before <= after).astype(BF16)
    left = rows[...]
    parts = []
    for _ in range(3):
        part = left.astype(BF16)
        parts.append(part)
        left = left - part.astype(F32)
    sums = jnp.dot(jnp.concatenate(parts, axis=0), upper, preferred_element_type=F32)
    sums = sums[:16] + (sums[16:32] + sums[32:])
    first = jnp.where(core == 0, sums[0:HC], sums[HC : 2 * HC])
    second = jnp.where(core == 0, sums[2 * HC : 3 * HC], sums[3 * HC : 4 * HC])
    across = jnp.concatenate([first, second, jnp.zeros((2, TOK), F32)], axis=0)
    across_ref[...] = across
    cum_ref[...] = jnp.concatenate([across, jnp.zeros((DH - 8, TOK), F32)], axis=0).T


def make_pieces(ks, vs, cum_ref, layer, pieces_ref):
    states = []
    decays = jnp.zeros((SUB, DH), F32)
    slot = lax.broadcasted_iota(jnp.int32, (SUB, DH), 0)
    for h in range(HC):
        cols = slice(h * DH, (h + 1) * DH)
        lane = layer * HC + h
        ch = cum_ref[:, lane : lane + 1]
        last = ch[TOK - 1 : TOK]
        kt = (ks[:, cols].astype(F32) * jnp.exp(last - ch)).astype(BF16)
        state = lax.dot_general(kt, vs[:, cols], (((0,), (0,)), ((), ())), preferred_element_type=F32)
        states.append(state.reshape(NCHIP, SUB, DH))
        total = jnp.exp(last)
        high = total.astype(BF16).astype(F32)
        decays = jnp.where(slot == h, high, decays)
        decays = jnp.where(slot == HC + h, total - high, decays)
    states.append(jnp.broadcast_to(decays[None], (NCHIP, SUB, DH)))
    pieces_ref[...] = jnp.concatenate(states, axis=1).astype(BF16)


def make_intra(qs, ks, vs, cum_ref, across_ref, layer, intra_ref):
    lower = lax.broadcasted_iota(jnp.int32, (BLK, BLK), 0) >= lax.broadcasted_iota(
        jnp.int32, (BLK, BLK), 1
    )
    for h in range(HC):
        cols = slice(h * DH, (h + 1) * DH)
        lane = layer * HC + h
        for i in range(2):
            rows = slice(i * BLK, (i + 1) * BLK)
            total = None
            for j in range(i + 1):
                keys = slice(j * BLK, (j + 1) * BLK)
                scores = lax.dot_general(
                    qs[rows, cols], ks[keys, cols], (((1,), (1,)), ((), ())),
                    preferred_element_type=F32,
                )
                spread = cum_ref[rows, lane : lane + 1] - across_ref[lane : lane + 1, keys]
                if i == j:
                    factor = jnp.where(lower, jnp.exp(jnp.where(lower, spread, 0.0)), 0.0)
                else:
                    factor = jnp.exp(spread)
                weights = (scores * factor).astype(BF16)
                part = jnp.dot(weights, vs[keys, cols], preferred_element_type=F32)
                total = part if total is None else total + part
            intra_ref[rows, cols] = total


def both_cores(core, mine_ref, yours_ref, out):
    out[span(core, BLK), :] = silu(mine_ref[...].astype(F32)).astype(BF16)
    out[span(1 - core, BLK), :] = silu(yours_ref[...].astype(F32)).astype(BF16)


HALF = pl.BlockSpec((BLK, HW), lambda _, place: (0, place[0]))


def first_state_kernel(
    place, k_ref, other_k_ref, v_ref, other_v_ref, decay_ref, other_decay_ref,
    pieces_ref, ks, vs, cum_ref, across_ref, rows,
):
    core = place[0]
    both_cores(core, k_ref, other_k_ref, ks)
    both_cores(core, v_ref, other_v_ref, vs)
    sum_decays(core, decay_ref, other_decay_ref, cum_ref, across_ref, rows)
    make_pieces(ks, vs, cum_ref, 0, pieces_ref)


IN_VMEM = pl.BlockSpec(memory_space=pltpu.VMEM)
ANY = pl.BlockSpec(memory_space=pl.ANY)
HEADS_OUT = pltpu.HBM((TOK, HW), BF16)
QUERY_OUT = struct((TOK, HW), BF16)
INTRA_OUT = struct((TOK, HW), F32)
WO_OUT = pltpu.VMEM((2 * HW, NHEAD * WIDTH), BF16)
WKV_OUT = pltpu.VMEM((2, NHEAD * WIDTH // 2, 2 * HW), BF16)
PIECES_OUT = struct((NCHIP, PIECE, DH), BF16)


def first_state(place, *args):
    outs = (PIECES_OUT, QUERY_OUT, QUERY_OUT, struct((TOK, DH), F32), struct((8, TOK), F32))
    scratch = (pltpu.VMEM((16, TOK), F32),)
    specs = [HALF] * 4 + [whole(a.shape) for a in args[4:]]
    return call(
        first_state_kernel, "first_state", place, args, outs, in_specs=specs, scratch=scratch
    )


def first_intra_kernel(
    place, q_ref, other_ref, ks, vs, cum_ref, across_ref, intra_ref, qs
):
    core = place[0]
    both_cores(core, q_ref, other_ref, qs)
    make_intra(qs, ks, vs, cum_ref, across_ref, 0, intra_ref)


def first_intra(place, q, other, ks, vs, cum, across):
    args = (q, other, ks, vs, cum, across)
    specs = [HALF] * 2 + [whole(a.shape) for a in args[2:]]
    outs = (INTRA_OUT, QUERY_OUT)
    return call(first_intra_kernel, "first_intra", place, args, outs, in_specs=specs)


def gained(h_ref, gain_ref):
    parts = []
    total = None
    for i in range(QUAD):
        wide = h_ref[i].astype(F32)
        parts.append((wide * gain_ref[i]).astype(BF16))
        for n in range(WIDTH // DH):
            tile = wide[:, n * DH : (n + 1) * DH]
            total = tile * tile if total is None else total + tile * tile
    return jnp.concatenate(parts, axis=1), total


def project_step(h_refs, w, gain_ref, acc, square):
    step = pl.program_id(0)
    parts, totals = zip(*(gained(h_ref, gain_ref) for h_ref in h_refs))
    part, total = jnp.concatenate(parts, axis=0), jnp.concatenate(totals, axis=0)

    term = jnp.dot(part, w, preferred_element_type=F32)

    @pl.when(step == 0)
    def _():
        square[...] = total
        acc[...] = term

    @pl.when(step > 0)
    def _():
        square[...] += total
        acc[...] += term


def row_scale(square):
    mean = jnp.sum(square, axis=-1, keepdims=True) / (NHEAD * WIDTH)
    return lax.rsqrt(mean + 1e-06)


def chunk_at(i, place):
    return jnp.where(i == 0, place[1], 1 - place[1]), 0, 0


def projection_specs(width):
    return (
        pl.BlockSpec((QUAD, BLK, WIDTH), chunk_at),
        pl.BlockSpec((1, QUAD * WIDTH, width), lambda i, _: (i, 0, 0)),
        pl.BlockSpec((QUAD, 1, WIDTH), chunk_at),
    )


def own_kv_kernel(place, h_ref, w_ref, gain_ref, out_ref, held, acc, square, sems):
    step = pl.program_id(0)
    fetches = [
        pltpu.make_async_copy(w_ref.at[n], held.at[n], sems.at[n]) for n in range(PAIR)
    ]

    @pl.when(step == 0)
    def _():
        for fetch in fetches:
            fetch.start()
        fetches[0].wait()

    @pl.when(step == 1)
    def _():
        fetches[1].wait()

    project_step([h_ref], held[step], gain_ref, acc, square)

    @pl.when(step == PAIR - 1)
    def _():
        out_ref[...] = silu(acc[...] * row_scale(square[...])).astype(BF16)


def own_kv(place, h, w, gain):
    hs, _, gs = projection_specs(2 * HW)
    return call(
        own_kv_kernel, "own_kv", place, (h, in_hbm(w), gain),
        (struct((BLK, 2 * HW), BF16), WKV_OUT),
        grid=(PAIR,), in_specs=[hs, ANY, gs], out_specs=[whole((BLK, 2 * HW)), IN_VMEM],
        scratch=(
            pltpu.VMEM((BLK, 2 * HW), F32), pltpu.VMEM((BLK, DH), F32),
            pltpu.SemaphoreType.DMA((PAIR,)),
        ),
    )


def second_state_kernel(
    place, h_ref, w_ref, gain_ref, own_ref, cum_ref, pieces_ref, ks, vs, acc, square
):
    core = place[0]
    project_step([h_ref], w_ref[pl.program_id(0)], gain_ref, acc, square)

    @pl.when(pl.program_id(0) == PAIR - 1)
    def _():
        scale = row_scale(square[...])
        for n, dst in enumerate((ks, vs)):
            cols = slice(n * HW, (n + 1) * HW)
            dst[span(core, BLK), :] = own_ref[:, cols]
            dst[span(1 - core, BLK), :] = silu(acc[:, cols] * scale).astype(BF16)
        make_pieces(ks, vs, cum_ref, 1, pieces_ref)


def second_state(place, h, w, gain, own, cum):
    hs, _, gs = projection_specs(2 * HW)
    return call(
        second_state_kernel, "second_state", place, (h, w, gain, own, cum),
        (PIECES_OUT, HEADS_OUT, HEADS_OUT),
        grid=(PAIR,), in_specs=[hs, IN_VMEM, gs, whole(own.shape), whole(cum.shape)],
        scratch=(pltpu.VMEM((BLK, 2 * HW), F32), pltpu.VMEM((BLK, DH), F32)),
    )


def second_intra_kernel(
    place, mine_ref, yours_ref, w_ref, gain_ref, ks, vs, cum_ref, across_ref,
    intra_ref, qs, acc, square,
):
    core = place[0]
    project_step([mine_ref, yours_ref], w_ref[0], gain_ref, acc, square)

    @pl.when(pl.program_id(0) == PAIR - 1)
    def _():
        act = silu(acc[...] * row_scale(square[...])).astype(BF16)
        qs[span(core, BLK), :] = act[:BLK]
        qs[span(1 - core, BLK), :] = act[BLK:]
        make_intra(qs, ks, vs, cum_ref, across_ref, 1, intra_ref)


def second_intra(place, mine, yours, w, gain, ks, vs, cum, across):
    hs, ws, gs = projection_specs(HW)
    return call(
        second_intra_kernel, "second_intra", place,
        (mine, yours, in_hbm(w), gain, in_hbm(ks), in_hbm(vs), cum, in_hbm(across)),
        (pltpu.HBM((TOK, HW), F32), HEADS_OUT),
        grid=(PAIR,),
        in_specs=[hs, hs, ws, gs] + [whole(a.shape) for a in (ks, vs, cum, across)],
        scratch=(pltpu.VMEM((TOK, HW), F32), pltpu.VMEM((TOK, DH), F32)),
    )


def cut_kernel(place, k_ref, v_ref, q_ref, both_ref, give_ref):
    core = place[0]
    for n, src in enumerate((k_ref, v_ref, q_ref)):
        both_ref[:, n * HW : (n + 1) * HW] = src[:, span(core, HW)]
        give = src[:, span(1 - core, HW)]
        both_ref[:, (n + 3) * HW : (n + 4) * HW] = give
        give_ref[:, n * HW : (n + 1) * HW] = give


def cut(place, *weights):
    rows = weights[0].shape[0]
    outs = (struct((rows, 6 * HW), BF16), struct((rows, 3 * HW), BF16))
    return call(cut_kernel, "cut", place, [in_hbm(w) for w in weights], outs)


def pack_kernel(place, near_ref, near_other_ref, far_ref, far_other_ref, kv_ref, wq_ref):
    core = place[0]
    rows = near_ref.shape[0]
    for n, pair in enumerate(((near_ref, near_other_ref), (far_ref, far_other_ref))):
        for src, owner in zip(pair, (core, 1 - core)):
            at = pl.ds(pl.multiple_of(owner * rows, rows), rows)
            kv_ref[n, at, :] = src[:, : 2 * HW]
            wq_ref[n, at, :] = src[:, 2 * HW : 3 * HW]


def pack(place, *parts):
    rows = 2 * parts[0].shape[0]
    outs = (pltpu.HBM((2, rows, 2 * HW), BF16), pltpu.HBM((2, rows, HW), BF16))
    return call(pack_kernel, "pack", place, parts, outs)


def scan_kernel(place, in_ref, out_ref):
    states = [jnp.zeros((SUB, DH), F32) for _ in range(HC)]
    empty = jnp.zeros((PIECE - HC * SUB, DH), F32)
    for p in range(NCHIP):
        piece = in_ref[p].astype(F32)
        out_ref[p] = jnp.concatenate(states + [empty], axis=0).astype(BF16)
        decays = piece[HC * SUB :]
        for h in range(HC):
            decay = decays[h : h + 1] + decays[HC + h : HC + h + 1]
            states[h] = states[h] * decay + piece[h * SUB : (h + 1) * SUB]


def scan(place, pieces):
    return call(scan_kernel, "scan", place, (pieces,), (PIECES_OUT,))[0]


def finish_kernel(
    layer, place, pieces_ref, cum_ref, intra_hbm, qs_hbm, gain_hbm, wo_ref,
    mine_ref, yours_ref, held, out, intra_ref, qs_ref, gain_ref, sems,
):
    core = place[0]
    pairs = ((intra_hbm, intra_ref), (qs_hbm, qs_ref), (gain_hbm, gain_ref), (wo_ref, held))
    fetches = [pltpu.make_async_copy(a, b, sems.at[n]) for n, (a, b) in enumerate(pairs)]
    for fetch in fetches:
        fetch.start()
    pieces = pieces_ref[...].astype(F32)
    states = [
        pieces[:, h * SUB : (h + 1) * SUB].reshape(DH, DH).astype(BF16) for h in range(HC)
    ]
    scales = [jnp.exp(cum_ref[:, layer * HC + h : layer * HC + h + 1]) for h in range(HC)]
    for fetch in fetches[:3]:
        fetch.wait()
    for h in range(HC):
        cols = slice(h * DH, (h + 1) * DH)
        carried = jnp.dot(qs_ref[:, cols], states[h], preferred_element_type=F32)
        att = intra_ref[:, cols] + carried * scales[h]
        square = jnp.mean(att * att, axis=-1, keepdims=True)
        gain = gain_ref[pl.ds(core * HC + h, 1), :]
        out[:, cols] = (att * lax.rsqrt(square + 1e-06) * gain).astype(BF16)
    mine_ref[...] = out[span(core, BLK), :]
    yours_ref[...] = out[span(1 - core, BLK), :]
    fetches[3].wait()


def finish(place, layer, pieces, intra, cum, qs, gain, wo):
    if layer:
        intra, qs = in_hbm(intra), in_hbm(qs)
    return call(
        lambda *refs: finish_kernel(layer, *refs), "finish", place,
        (pieces, cum, intra, qs, gain, in_hbm(wo)),
        (struct((BLK, HW), BF16), struct((BLK, HW), BF16), WO_OUT),
        in_specs=[whole(pieces.shape), whole(cum.shape)] + [ANY] * 4,
        out_specs=[whole((BLK, HW)), whole((BLK, HW)), IN_VMEM],
        scratch=(
            pltpu.VMEM((TOK, HW), BF16), pltpu.VMEM((TOK, HW), F32), pltpu.VMEM((TOK, HW), BF16),
            pltpu.VMEM((2 * HC, DH), F32), pltpu.SemaphoreType.DMA((4,)),
        ),
    )


def project_kernel(place, mine_ref, yours_ref, w_ref, out_ref, rows):
    core = place[0]

    @pl.when(pl.program_id(0) == 0)
    def _():
        rows[:, span(core, HW)] = mine_ref[...]
        rows[:, span(1 - core, HW)] = yours_ref[...]

    cols = span(pl.program_id(0), KSTEP)
    term = jnp.dot(rows[...], w_ref[:, cols], preferred_element_type=F32).astype(BF16)
    for i in range(NHEAD // STEPS):
        out_ref[i] = term[:, i * WIDTH : (i + 1) * WIDTH]


def project(place, mine, yours, w):
    return call(
        project_kernel, "project", place, (mine, yours, w),
        (struct((NHEAD, BLK, WIDTH), BF16),),
        grid=(STEPS,),
        in_specs=[
            whole(mine.shape), whole(yours.shape),
            IN_VMEM,
        ],
        out_specs=[pl.BlockSpec((NHEAD // STEPS, BLK, WIDTH), lambda i, _: (i, 0, 0))],
        scratch=(pltpu.VMEM((BLK, 2 * HW), BF16),),
        flops=2 * BLK * 2 * HW * NHEAD * WIDTH,
    )[0]


def exchange(parts, axes):
    return lax.all_to_all(parts, axes, 0, 0)


def after(value, *others):
    return lax.optimization_barrier((value, *others))[0]


def rest(place, layer, before, intra, cum, qs, gain, w):
    mine, yours, w = finish(place, layer, before, intra, cum, qs, in_hbm(gain.reshape(2 * HC, DH)), w)
    yours = lax.ppermute(yours, "c", SWAP)
    terms = exchange(project(place, mine, yours, w), ("x", "yl"))
    return jnp.sum(terms.astype(F32), axis=0)


def local(
    q1, k1, v1, decay1, gain_out1, wo1, stream_in, gain_in2, wq2, wk2, wv2, decay2, gain_out2, wo2
):
    core = lax.axis_index("c")
    place = jnp.stack([core, lax.axis_index("yh")]).astype(jnp.int32)

    def swapped(*arrays):
        return [lax.ppermute(a, "c", SWAP) for a in arrays]

    decays = jnp.concatenate([decay1.T, decay2.T], axis=0)
    other_k, other_v, other_decays = swapped(k1, v1, decays)
    pieces, ks, vs, cum, across = first_state(
        place, in_hbm(k1), other_k, in_hbm(v1), other_v, decays, other_decays
    )

    near, give = cut(place, wk2, wv2, wq2)
    far = lax.ppermute(near, "yh", SWAP)
    far = after(far, pieces)
    near_other, far_other = swapped(give, far[:, 3 * HW :])
    rows_kv, rows_q = pack(place, near, near_other, far, far_other)
    q1 = after(q1, pieces)
    other_q, = swapped(q1)
    sums, _, rows_kv, rows_q = lax.optimization_barrier(
        (exchange(pieces, ("yh", "z")), other_q, rows_kv, rows_q)
    )
    before = exchange(scan(place, sums), ("yh", "z"))

    def gather(rows):
        return lax.all_gather(rows, "z", axis=1, tiled=True)

    wkv = gather(rows_kv)
    intra, qs = first_intra(place, q1, other_q, ks, vs, cum, across)
    first_share = rest(place, 0, before, intra, cum, qs, gain_out1, wo1)
    stream = (stream_in.astype(F32) + first_share).astype(BF16)
    wq = gather(after(rows_q, stream))

    mine = exchange(jnp.broadcast_to(stream[None], (NHEAD, BLK, WIDTH)), ("x", "yl"))
    yours = lax.ppermute(mine, "c", SWAP)
    gain = gain_in2.reshape(NHEAD, 1, WIDTH)
    own, wkv = own_kv(place, mine, wkv, gain)
    pieces, ks, vs = second_state(place, yours, wkv, gain, own, cum)
    sums = exchange(pieces, ("yh", "z"))
    before = exchange(scan(place, sums), ("yh", "z"))
    intra, qs = second_intra(place, mine, yours, wq, gain, ks, vs, cum, across)
    second_share = rest(place, 1, before, intra, cum, qs, gain_out2, wo2)
    return (stream.astype(F32) + second_share).astype(BF16)


def solution(mesh):
    fine = Mesh(mesh.devices.reshape(2, 8, 2, 4, 2), ("yh", "z", "c", "x", "yl"))
    seq, head = ("yh", "z", "c"), ("x", "yl")
    both = P(seq, head)
    placed = (
        both, both, both, both, P(head), P(head, None), both, P(),
        both, both, both, both, P(head), P(head, None),
    )
    return jax.shard_map(local, mesh=fine, in_specs=placed, out_specs=both, check_vma=False)
```
